256 devices in a mesh: pts: 128 (over z_hi, y, x, core), ch: 2 (over z_lo).
Axes of the slice: x: 4, y: 4, z: 8 (z_hi: 4, z_lo: 2; z = z_hi * 2 + z_lo), core: 2. Of those that a mesh axis runs over, the one named last changes fastest.
Arguments:
- points: bfloat16 [524288, 256], P('pts', 'ch'), may hold values from -6 to 6
- order: int32 [524288], P('pts'), may hold values from 0 to 4095, as said below
- norm_gain: float32 [256], P('ch'), may hold values from 0.4 to 12
- qkv_weight: bfloat16 [3, 256, 256], replicated, may hold values from -0.375 to 0.375
- out_weight: bfloat16 [256, 256], replicated, may hold values from -0.375 to 0.375
- tree_gain: float32 [4, 256], P(None, 'ch'), may hold values from 0.3 to 1.5
- partner_slot: int32 [2048, 4], P('pts'), may hold values from 0 to 15
- cotangent: bfloat16 [524288, 256], P('pts', 'ch'), may hold values from -6 to 6
Outputs:
- mixed: bfloat16 [524288, 256], P('pts', 'ch')
- point_grad: bfloat16 [524288, 256], P('pts', 'ch')
- qkv_grad: float32 [3, 256, 256], P(None, None, 'ch')
- out_grad: float32 [256, 256], P('ch')
The draws below stay inside these ranges and needn't reach their ends.
Inputs may be any that keep to these rules, and one draw needn't show every extreme that they name: `order`: each aligned block of 4096 entries is a permutation of 0 to 4095.
All inputs are finite; a program needn't handle non-finite values.
Results may differ from the reference program's by a relative error of at most 0.015.
The reference program's roundings to bfloat16 on the way (of `normed`, `probs_half`, `attended`, `hidden_grad` and `attended_grad`) count: a program that leaves them out, or rounds other values in their place, can miss the bound.
Values may be sent and summed in bfloat16 or wider, within the bound.
A program may use at most 128 MiB of HBM per device.

```python
import math
import jax
import jax.numpy as jnp
from jax import lax

D = 256
HEAD = 32
BALL = 256
P_DEV = 4096
LEVELS = 4
POINTS = 524288
NODES = 2048
N_PTS = 128


def draw_order(key, part):
    key = jax.random.fold_in(key, 11)
    keys = jax.random.split(key, POINTS // P_DEV)
    perms = jax.vmap(lambda one_key: jax.random.permutation(one_key, P_DEV))(keys)
    return perms.reshape(-1).astype(jnp.int32)


def rising_gain(key, ramp):
    position = jnp.arange(D, dtype=jnp.float32) / (D - 1)
    jitter = jax.random.uniform(key, (D,), jnp.float32, 0.8, 1.25)
    return 0.6 * jnp.exp(position * jnp.log(ramp)) * jitter


def draw_norm_gain(key, part):
    key = jax.random.fold_in(key, 23)
    base = rising_gain(key, 8.0)
    return base.astype(jnp.float32)


def touch_ends(array, rng, low, top_value):
    shape = array.shape
    index_at = [jax.random.randint(jax.random.fold_in(rng, axis), (), 0, shape[axis]) for axis in range(len(shape))]
    array = array.at[tuple(index_at)].set(low)
    longest = shape.index(max(shape))
    index_at[longest] = (index_at[longest] + 1) % shape[longest]
    return array.at[tuple(index_at)].set(top_value)


def block_levels(own_key, shape, shards, low, largest):
    level, own = 1.0, jax.random.fold_in(own_key, 6)
    for dim, blocks in shards:
        heights = jnp.exp(jax.random.uniform(jax.random.fold_in(own, dim), (blocks,), jnp.float32, low / len(shards), largest / len(shards)))
        level = level * jnp.repeat(heights, shape[dim] // blocks).reshape([-1 if axis == dim else 1 for axis in range(len(shape))])
    return level


def noise(rng, extent, width, most, cuts=(), held_as=jnp.bfloat16):
    level = block_levels(rng, extent, cuts, -0.22, 0.18) if cuts else 1.0
    entries = jax.random.normal(rng, extent, jnp.float32) * width * level
    return jnp.minimum(jnp.maximum(entries, -most), most).astype(held_as)


def setup_inputs(seed: int = 0) -> dict:
    key_list = jax.random.split(jax.random.key(seed), 9)
    points = noise(key_list[0], (POINTS, D), 1.0, 6.0, ((0, 128), (1, 2)))
    order = draw_order(jax.random.fold_in(key_list[8], 71), 0)
    norm_gain = draw_norm_gain(jax.random.fold_in(key_list[8], 71), 0)
    qkv_weight = noise(key_list[3], (3, D, D), D ** -0.5, 0.375)
    out_weight = noise(key_list[4], (D, D), D ** -0.5, 0.375)
    tree_gain = jnp.clip(jnp.exp(math.log(1.5) - 1.60943787 * jax.random.uniform(key_list[5], (LEVELS, D), jnp.float32) ** block_levels(key_list[5], (LEVELS, D), ((1, 2),), -0.2, 0.2)), 0.3, 1.5)
    partner_slot = touch_ends(jax.random.randint(key_list[6], (NODES, LEVELS), 0, P_DEV // BALL), jax.random.fold_in(key_list[6], 1), 0, (P_DEV // BALL) - 1).astype(jnp.int32)
    cotangent = noise(key_list[7], (POINTS, D), 1.0, 6.0, ((0, 128), (1, 2)))
    return {"points": points, "order": order, "norm_gain": norm_gain, "qkv_weight": qkv_weight, "out_weight": out_weight, "tree_gain": tree_gain, "partner_slot": partner_slot, "cotangent": cotangent}


EPSILON = 1e-06

def softmax_rows(scores):
    shifted = scores - lax.optimization_barrier(jnp.max(scores, axis=-1, keepdims=True))
    weights = jnp.exp(shifted)
    return weights / lax.optimization_barrier(jnp.sum(weights, axis=-1, keepdims=True))

def to_heads(rows_in):
    return rows_in.astype(jnp.float32).reshape(rows_in.shape[0] // BALL, BALL, -1, HEAD)

def attend(query_rows, key_rows, value_rows):
    queries = to_heads(query_rows)
    keyset = to_heads(key_rows)
    values_in = to_heads(value_rows)
    scores = jnp.einsum('bqhd,bkhd->bhqk', queries, keyset) * HEAD ** (-0.5)
    probs_half = softmax_rows(scores).astype(jnp.bfloat16).astype(jnp.float32)
    result = jnp.einsum('bhqk,bkhd->bqhd', probs_half, values_in)
    return result.reshape(query_rows.shape).astype(jnp.bfloat16)

def attend_back(query_rows, key_rows, value_rows, grad_rows):
    queries = to_heads(query_rows)
    keyset = to_heads(key_rows)
    values_in = to_heads(value_rows)
    grad_heads = to_heads(grad_rows)
    scores = jnp.einsum('bqhd,bkhd->bhqk', queries, keyset) * HEAD ** (-0.5)
    probs = softmax_rows(scores)
    probs_half = probs.astype(jnp.bfloat16).astype(jnp.float32)
    probs_grad = jnp.einsum('bqhd,bkhd->bhqk', grad_heads, values_in)
    value_grad = jnp.einsum('bhqk,bqhd->bkhd', probs_half, grad_heads)
    score_grad = probs * (probs_grad - lax.optimization_barrier(jnp.sum(probs_grad * probs, axis=-1, keepdims=True)))
    score_half = (score_grad * HEAD ** (-0.5)).astype(jnp.bfloat16).astype(jnp.float32)
    query_grad = jnp.einsum('bhqk,bkhd->bqhd', score_half, keyset)
    key_grad = jnp.einsum('bhqk,bqhd->bkhd', score_half, queries)
    shape_out = query_rows.shape
    return (query_grad.reshape(shape_out).astype(jnp.bfloat16), key_grad.reshape(shape_out).astype(jnp.bfloat16), value_grad.reshape(shape_out).astype(jnp.bfloat16))

def block_forward(block_points, block_order, norm_gain, qkv_weight, out_weight):
    ordered = jnp.take(block_points, block_order, axis=0).astype(jnp.float32)
    inverse_rms = lax.rsqrt(lax.optimization_barrier(jnp.mean(ordered * ordered, axis=-1, keepdims=True)) + EPSILON)
    normed = (ordered * inverse_rms * norm_gain).astype(jnp.bfloat16)
    projected = [jnp.dot(normed, qkv_weight[proj_index], preferred_element_type=jnp.float32).astype(jnp.bfloat16) for proj_index in range(3)]
    attended = attend(projected[0], projected[1], projected[2])
    hidden = ordered + jnp.dot(attended, out_weight, preferred_element_type=jnp.float32)
    return (ordered, inverse_rms, normed, projected, attended, hidden)

def partner_index(slots, level):
    balls_dev = P_DEV // BALL
    node_ids = jnp.arange(slots.shape[0], dtype=jnp.int32)
    owners = node_ids // balls_dev
    return (jnp.bitwise_xor(owners, 1 << level) * balls_dev + slots[:, level]).astype(jnp.int32)

def silu_slope(values):
    sigma = jax.nn.sigmoid(values)
    return sigma * (1.0 + values * (1.0 - sigma))

def reference(points, order, norm_gain, qkv_weight, out_weight, tree_gain, partner_slot, cotangent):
    block_points = points.reshape(N_PTS, P_DEV, D)
    block_order = order.reshape(N_PTS, P_DEV)

    def hidden_only(pair):
        return block_forward(pair[0], pair[1], norm_gain, qkv_weight, out_weight)[5]
    hidden = lax.map(hidden_only, (block_points, block_order))
    states = hidden.reshape(NODES, BALL, D).sum(axis=1) * BALL ** (-0.5)
    chosen_list = []
    for level in range(LEVELS):
        partner = partner_index(partner_slot, level)
        chosen = states[partner]
        chosen_list.append((partner, chosen))
        states = states + tree_gain[level] * jax.nn.silu(chosen)
    mixed = (hidden.reshape(NODES, BALL, D) + states[:, None, :]).reshape(POINTS, D).astype(jnp.bfloat16)
    cot_full = cotangent.astype(jnp.float32)
    node_grad = cot_full.reshape(NODES, BALL, D).sum(axis=1)
    for level in reversed(range(LEVELS)):
        partner, chosen = chosen_list[level]
        terms = tree_gain[level] * silu_slope(chosen) * node_grad
        node_grad = node_grad + jnp.zeros_like(node_grad).at[partner].add(terms)
    hidden_grad = cot_full.reshape(NODES, BALL, D) + node_grad[:, None, :] * BALL ** (-0.5)
    hidden_grad = hidden_grad.reshape(N_PTS, P_DEV, D).astype(jnp.bfloat16)

    def backward_block(carry, triple):
        qkv_total, out_total = carry
        one_points, one_order, grad_half = triple
        ordered, inverse_rms, normed, projected, attended, unused_hidden = block_forward(one_points, one_order, norm_gain, qkv_weight, out_weight)
        out_term = jnp.dot(attended.T, grad_half, preferred_element_type=jnp.float32)
        attended_grad = jnp.dot(grad_half, out_weight.T, preferred_element_type=jnp.float32).astype(jnp.bfloat16)
        grads = attend_back(projected[0], projected[1], projected[2], attended_grad)
        qkv_term = jnp.stack([jnp.dot(normed.T, grads[proj_index], preferred_element_type=jnp.float32) for proj_index in range(3)])
        normed_grad = sum((jnp.dot(grads[proj_index], qkv_weight[proj_index].T, preferred_element_type=jnp.float32) for proj_index in range(3)))
        correction = lax.optimization_barrier(jnp.sum(ordered * norm_gain * normed_grad, axis=-1, keepdims=True))
        ordered_grad = grad_half.astype(jnp.float32) + inverse_rms * norm_gain * normed_grad - ordered * inverse_rms ** 3 * correction / D
        grad_block = jnp.zeros((P_DEV, D), jnp.bfloat16).at[one_order].set(ordered_grad.astype(jnp.bfloat16))
        return ((qkv_total + qkv_term, out_total + out_term), grad_block)
    start = (jnp.zeros((3, D, D), jnp.float32), jnp.zeros((D, D), jnp.float32))
    totals, grad_blocks = lax.scan(backward_block, start, (block_points, block_order, hidden_grad))
    return (mixed, grad_blocks.reshape(POINTS, D), totals[0], totals[1])
```

```python
import math

import jax
import jax.numpy as jnp
from jax import lax
from jax.experimental import pallas as pl
from jax.experimental.pallas import tpu as pltpu
from jax.sharding import PartitionSpec as P

HEAD = 32
BALL = 256
LEVELS = 4
EPSILON = 1e-06

ROWS = 4096
HALF = 2048
LOCAL = 128
WIDTH = 256
HEADS = 8
BALLS = 8
GROUP = 16

F32 = jnp.float32
BF16 = jnp.bfloat16
MESH = pl.DeviceIdType.MESH
SCALE = HEAD ** (-0.5)
SCALE_LOG2 = SCALE * math.log2(math.e)


def nn(left, right):
    return lax.dot_general(left, right, (((1,), (0,)), ((), ())), preferred_element_type=F32)


def nt(left, right):
    return lax.dot_general(left, right, (((1,), (1,)), ((), ())), preferred_element_type=F32)


def tn(left, right):
    return lax.dot_general(left, right, (((0,), (0,)), ((), ())), preferred_element_type=F32)


def gather_kernel(order_ref, points_ref, out_ref, wide, moved):
    wide[...] = points_ref[...].astype(F32)

    def step(block, carry):
        base = block * 16
        for inner in range(16):
            row = order_ref[base + inner]
            moved[pl.ds(base + inner, 1), :] = wide[pl.ds(row, 1), :]
        return carry

    lax.fori_loop(0, ROWS // 16, step, 0)
    out_ref[...] = moved[...].astype(BF16)


def scatter_kernel(order_ref, rows_ref, out_ref, wide, moved):
    wide[...] = rows_ref[...].astype(F32)

    def step(block, carry):
        base = block * 16
        for inner in range(16):
            row = order_ref[base + inner]
            moved[pl.ds(row, 1), :] = wide[pl.ds(base + inner, 1), :]
        return carry

    lax.fori_loop(0, ROWS // 16, step, 0)
    out_ref[...] = moved[...].astype(BF16)


def permute_rows(kernel, order, rows):
    return pl.pallas_call(
        kernel,
        out_shape=jax.ShapeDtypeStruct((ROWS, LOCAL), BF16),
        in_specs=[pl.BlockSpec(memory_space=pltpu.SMEM), pl.BlockSpec(memory_space=pltpu.VMEM)],
        out_specs=pl.BlockSpec(memory_space=pltpu.VMEM),
        scratch_shapes=[pltpu.VMEM((ROWS, LOCAL), F32), pltpu.VMEM((ROWS, LOCAL), F32)],
        compiler_params=pltpu.CompilerParams(vmem_limit_bytes=24 * 1024 * 1024),
    )(order, rows)


def exact_dot(dot, onehot, values):
    high = values.astype(BF16)
    rest = values - high.astype(F32)
    middle = rest.astype(BF16)
    low = (rest - middle.astype(F32)).astype(BF16)
    return dot(onehot, high) + dot(onehot, middle) + dot(onehot, low)


def main_kernel(
    gathered, cot, small, slots, w, wo,
    mixed, grads, total,
    xh, cth, sm, wt, kn, vn, q_t, k_t, v_t, att_t, nrm, hid, inv, probs, dx,
    tree, final_state, final_grad, mstage, gstage, acc_t,
    acc, recv_a, sum_a, recv_b, sum_b, recv_c, sum_c, recv_d, sum_d, all_e, all_f,
    s_small, s_pts, s_cot, s_mix, s_grad, s_tree, s_a, s_b, s_c, s_d, s_e, s_f, s_g,
):
    p = lax.axis_index("pts")
    c = lax.axis_index("ch")
    core = p % 2
    plane = (p // 2) % 16
    depth = p // 32
    other_c = 1 - c
    me = (p % GROUP) * 2 + c
    group_base = (p // GROUP) * GROUP
    pair = (p, other_c)
    sibling = (p + 1 - 2 * core, c)

    def tree_peer(distance):
        there = (me + distance) % 32
        return (group_base + there // 2, there % 2)

    def plane_index(distance):
        return (plane + distance) % 16

    def plane_peer(distance):
        return (depth * 32 + plane_index(distance) * 2 + core, c)

    def depth_index(distance):
        return (depth + distance) % 4

    def depth_peer(distance):
        return (depth_index(distance) * 32 + plane * 2 + core, c)

    barrier = pltpu.get_barrier_semaphore()
    for distance in range(1, 32):
        pl.semaphore_signal(barrier, inc=1, device_id=tree_peer(distance), device_id_type=MESH)
    far_base = (1 - plane // 8) * 8
    for step in range(8):
        far = (depth * 32 + (far_base + step) * 2 + core, c)
        pl.semaphore_signal(barrier, inc=1, device_id=far, device_id_type=MESH)
    for distance in range(1, 4):
        pl.semaphore_signal(barrier, inc=1, device_id=depth_peer(distance), device_id_type=MESH)

    own_rows = pl.ds(pl.multiple_of(c * HALF, HALF), HALF)
    xh[pl.ds(c, 1)] = gathered[own_rows, :][None]
    cth[pl.ds(c, 1)] = cot[own_rows, :][None]
    sm[pl.ds(c, 1)] = small[...][None]
    for index in range(3):
        wt[index] = jnp.transpose(w[index])

    pl.semaphore_wait(barrier, 42)

    def send(src, dst, sems, index, target):
        return pltpu.make_async_remote_copy(
            src_ref=src, dst_ref=dst, send_sem=sems.at[0, index], recv_sem=sems.at[1, index],
            device_id=target, device_id_type=MESH,
        )

    def theirs(ball):
        return pl.ds(pl.multiple_of(other_c * HALF + ball * BALL, BALL), BALL)

    def ours(ball):
        return pl.ds(pl.multiple_of(c * HALF + ball * BALL, BALL), BALL)

    def here(ball):
        return pl.ds(pl.multiple_of(ball * BALL, BALL), BALL)

    def small_copy():
        return send(small, sm.at[c], s_small, 0, pair)

    def points_copy(ball):
        return send(gathered.at[theirs(ball)], xh.at[c, here(ball)], s_pts, ball, pair)

    def cot_copy(ball):
        return send(cot.at[theirs(ball)], cth.at[c, here(ball)], s_cot, ball, pair)

    def mixed_copy(ball):
        return send(mstage.at[other_c, here(ball)], mixed.at[ours(ball)], s_mix, ball, pair)

    def grad_copy(ball):
        return send(gstage.at[other_c, here(ball)], grads.at[ours(ball)], s_grad, ball, pair)

    small_copy().start()
    for ball in range(BALLS):
        points_copy(ball).start()
    small_copy().wait_recv()
    gain = jnp.concatenate([sm[0, 0:1, :], sm[1, 0:1, :]], axis=1)

    node_row = pl.multiple_of(me * BALLS, BALLS)

    def both(ref, rows):
        return jnp.concatenate([ref[0, rows, :], ref[1, rows, :]], axis=1).astype(F32)

    def forward(ball, carry):
        rows = here(ball)
        points_copy(ball).wait_recv()
        cot_copy(ball).start()
        ordered = both(xh, rows)
        mean = jnp.sum(ordered * ordered, axis=1, keepdims=True) * (1.0 / WIDTH)
        inverse = lax.rsqrt(mean + EPSILON)
        inv[rows, :] = jnp.broadcast_to(inverse, (BALL, LOCAL))
        normed = (ordered * inverse * gain).astype(BF16)
        nrm[rows, :] = normed
        keyset = nn(normed, w[1]).astype(BF16)
        kn[rows, :] = keyset
        vn[rows, :] = nn(normed, w[2]).astype(BF16)
        q_t[ball] = nt(wt[0], normed).astype(BF16)
        k_t[ball] = nt(wt[1], normed).astype(BF16)
        v_t[ball] = nt(wt[2], normed).astype(BF16)
        for head in range(HEADS):
            cols = slice(head * HEAD, (head + 1) * HEAD)
            scores = nn(kn[rows, cols], q_t[ball, cols, :])
            top = jnp.max(scores, axis=0, keepdims=True)
            weights = jnp.exp2((scores - top) * SCALE_LOG2)
            scaled = weights * (1.0 / jnp.sum(weights, axis=0, keepdims=True))
            probs[ball * HEADS + head] = scaled
            att_t[ball, cols, :] = nn(v_t[ball, cols, :], scaled.astype(BF16)).astype(BF16)
        hidden = ordered + nn(jnp.transpose(att_t[ball]), wo[...])
        hid[rows, :] = hidden
        tree[pl.ds(node_row + ball, 1), 0:WIDTH] = jnp.sum(hidden, axis=0, keepdims=True) * BALL ** (-0.5)
        return carry

    lax.fori_loop(0, BALLS, forward, 0)

    for ball in range(BALLS):
        cot_copy(ball).wait_recv()
        tree[pl.ds(node_row + ball, 1), WIDTH:2 * WIDTH] = jnp.sum(
            both(cth, here(ball)), axis=0, keepdims=True
        )
    tree[pl.ds(node_row, BALLS), 2 * WIDTH:] = slots[pl.ds(pl.multiple_of(c * BALLS, BALLS), BALLS), :]

    def tree_copy(distance):
        block = tree.at[pl.ds(node_row, BALLS)]
        return send(block, block, s_tree, distance, tree_peer(distance))

    for distance in range(1, 32):
        tree_copy(distance).start()
    for distance in range(1, 32):
        tree_copy(distance).wait_recv()

    nodes = GROUP * 16
    range_ids = lax.broadcasted_iota(jnp.int32, (nodes, 1), 0) // 16
    lane_ids = lax.broadcasted_iota(jnp.int32, (nodes, nodes), 1)
    states = tree[:, 0:WIDTH]
    onehots, chosen_list, tree_gains = [], [], []
    for level in range(LEVELS):
        slot = tree[:, 2 * WIDTH + level:2 * WIDTH + level + 1].astype(jnp.int32)
        bit = (range_ids // (1 << level)) % 2
        partner = (range_ids + (1 - 2 * bit) * (1 << level)) * 16 + slot
        onehot = jnp.where(lane_ids == partner, 1.0, 0.0).astype(BF16)
        tree_gain = jnp.concatenate([sm[0, 1 + level:2 + level, :], sm[1, 1 + level:2 + level, :]], axis=1)
        chosen = exact_dot(nn, onehot, states)
        states = states + tree_gain * (chosen * jax.nn.sigmoid(chosen))
        onehots.append(onehot)
        chosen_list.append(chosen)
        tree_gains.append(tree_gain)
    final_state[...] = states
    node_grad = tree[:, WIDTH:2 * WIDTH]
    for level in reversed(range(LEVELS)):
        chosen = chosen_list[level]
        sigma = jax.nn.sigmoid(chosen)
        slope = sigma * (1.0 + chosen * (1.0 - sigma))
        node_grad = node_grad + exact_dot(tn, onehots[level], tree_gains[level] * slope * node_grad)
    final_grad[...] = node_grad
    acc_t[...] = jnp.zeros_like(acc_t)

    def backward(ball, carry):
        rows = here(ball)
        mixed_rows = (hid[rows, :] + final_state[pl.ds(node_row + ball, 1), :]).astype(BF16)
        mstage[0, rows, :] = mixed_rows[:, :LOCAL]
        mstage[1, rows, :] = mixed_rows[:, LOCAL:]
        mixed_copy(ball).start()
        mixed[ours(ball), :] = mstage[pl.ds(c, 1), rows, :][0]
        shift = final_grad[pl.ds(node_row + ball, 1), :] * BALL ** (-0.5)
        hidden_grad = (both(cth, rows) + shift).astype(BF16)
        acc_t[3] += nn(att_t[ball], hidden_grad)
        att_grad = nt(wo[...], hidden_grad).astype(BF16)
        for head in range(HEADS):
            cols = slice(head * HEAD, (head + 1) * HEAD)
            prob = probs[ball * HEADS + head]
            head_grad = att_grad[cols, :]
            prob_grad = nn(vn[rows, cols], head_grad)
            dx[2, cols, :] = nt(head_grad, prob.astype(BF16)).astype(BF16)
            dots = jnp.sum(prob_grad * prob, axis=0, keepdims=True)
            score_grad = (prob * (prob_grad - dots) * SCALE).astype(BF16)
            dx[0, cols, :] = nn(k_t[ball, cols, :], score_grad).astype(BF16)
            dx[1, cols, :] = nt(q_t[ball, cols, :], score_grad).astype(BF16)
        normed = nrm[rows, :]
        for index in range(3):
            acc_t[index] += nn(dx[index], normed)
        normed_grad = nn(w[0], dx[0]) + nn(w[1], dx[1]) + nn(w[2], dx[2])
        scaled_grad = jnp.transpose(normed_grad) * gain
        ordered = both(xh, rows)
        inverse = jnp.concatenate([inv[rows, :], inv[rows, :]], axis=1)
        correction = jnp.sum(ordered * scaled_grad, axis=1, keepdims=True) * (1.0 / WIDTH)
        ordered_grad = (
            hidden_grad.astype(F32) + inverse * scaled_grad - ordered * (inverse * inverse * inverse) * correction
        ).astype(BF16)
        gstage[0, rows, :] = ordered_grad[:, :LOCAL]
        gstage[1, rows, :] = ordered_grad[:, LOCAL:]
        grad_copy(ball).start()
        grads[ours(ball), :] = gstage[pl.ds(c, 1), rows, :][0]
        return carry

    lax.fori_loop(0, BALLS, backward, 0)

    for index in range(3):
        part = jnp.transpose(acc_t[index])
        acc[0, index * 256:(index + 1) * 256, :] = part[:, :LOCAL]
        acc[1, index * 256:(index + 1) * 256, :] = part[:, LOCAL:]
    for half in range(2):
        band = slice(half * LOCAL, (half + 1) * LOCAL)
        acc[half, 768:896, :] = acc_t[3, band, :LOCAL]
        acc[half, 896:1024, :] = acc_t[3, band, LOCAL:]

    kept = pl.ds(pl.multiple_of(core * 512, 512), 512)
    given = pl.ds(pl.multiple_of((1 - core) * 512, 512), 512)
    copy_a = send(acc.at[:, given], recv_a, s_a, 0, sibling)
    copy_a.start()
    copy_a.wait_recv()
    sum_a[...] = acc[:, kept, :] + recv_a[...]
    copy_b = send(sum_a.at[other_c], recv_b, s_b, 0, pair)
    copy_b.start()
    copy_b.wait_recv()
    sum_b[...] = sum_a[pl.ds(c, 1)][0] + recv_b[...]

    def copy_c(distance):
        piece = pl.ds(pl.multiple_of(plane_index(distance) * 32, 32), 32)
        return send(sum_b.at[piece], recv_c.at[distance], s_c, distance, plane_peer(distance))

    for distance in range(1, 16):
        copy_c(distance).start()
    part = sum_b[pl.ds(pl.multiple_of(plane * 32, 32), 32), :]
    for distance in range(1, 16):
        copy_c(distance).wait_recv()
        part = part + recv_c[distance]
    sum_c[...] = part

    def copy_d(distance):
        piece = pl.ds(pl.multiple_of(depth_index(distance) * 8, 8), 8)
        return send(sum_c.at[piece], recv_d.at[distance], s_d, distance, depth_peer(distance))

    for distance in range(1, 4):
        copy_d(distance).start()
    part = sum_c[pl.ds(pl.multiple_of(depth * 8, 8), 8), :]
    for distance in range(1, 4):
        copy_d(distance).wait_recv()
        part = part + recv_d[distance]
    sum_d[...] = part

    depth_rows = pl.ds(pl.multiple_of(depth * 8, 8), 8)
    all_e[depth_rows, :] = part

    def copy_e(distance):
        return send(sum_d, all_e.at[depth_rows], s_e, distance, depth_peer(distance))

    for distance in range(1, 4):
        copy_e(distance).start()
    for distance in range(1, 4):
        copy_e(distance).wait_recv()

    plane_rows = pl.ds(pl.multiple_of(plane * 32, 32), 32)
    all_f[plane_rows, :] = all_e[...]

    def copy_f(distance):
        return send(all_e, all_f.at[plane_rows], s_f, distance, plane_peer(distance))

    for distance in range(1, 16):
        copy_f(distance).start()
    for distance in range(1, 16):
        copy_f(distance).wait_recv()

    copy_g = send(all_f, total.at[kept], s_g, 0, sibling)
    copy_g.start()
    total[kept, :] = all_f[...]
    copy_g.wait_recv()

    small_copy().wait_send()

    def settle(ball, carry):
        points_copy(ball).wait_send()
        cot_copy(ball).wait_send()
        mixed_copy(ball).wait()
        grad_copy(ball).wait()
        return carry

    lax.fori_loop(0, BALLS, settle, 0)
    for distance in range(1, 32):
        tree_copy(distance).wait_send()
    copy_a.wait_send()
    copy_b.wait_send()
    for distance in range(1, 16):
        copy_c(distance).wait_send()
        copy_f(distance).wait_send()
    for distance in range(1, 4):
        copy_d(distance).wait_send()
        copy_e(distance).wait_send()
    copy_g.wait_send()


def run_main(gathered, cot, small, slots, w, wo):
    vmem = pl.BlockSpec(memory_space=pltpu.VMEM)
    sems = lambda count: pltpu.SemaphoreType.DMA((2, count))
    v = pltpu.VMEM
    return pl.pallas_call(
        main_kernel,
        out_shape=(
            jax.ShapeDtypeStruct((ROWS, LOCAL), BF16),
            jax.ShapeDtypeStruct((ROWS, LOCAL), BF16),
            jax.ShapeDtypeStruct((1024, LOCAL), F32),
        ),
        in_specs=[vmem] * 6,
        out_specs=(vmem,) * 3,
        scratch_shapes=[
            v((2, HALF, LOCAL), BF16),
            v((2, HALF, LOCAL), BF16),
            v((2, 8, LOCAL), F32),
            v((3, WIDTH, WIDTH), BF16),
            v((HALF, WIDTH), BF16),
            v((HALF, WIDTH), BF16),
            v((BALLS, WIDTH, BALL), BF16),
            v((BALLS, WIDTH, BALL), BF16),
            v((BALLS, WIDTH, BALL), BF16),
            v((BALLS, WIDTH, BALL), BF16),
            v((HALF, WIDTH), BF16),
            v((HALF, WIDTH), F32),
            v((HALF, LOCAL), F32),
            v((BALLS * HEADS, BALL, BALL), F32),
            v((3, WIDTH, BALL), BF16),
            v((256, 640), F32),
            v((256, WIDTH), F32),
            v((256, WIDTH), F32),
            v((2, HALF, LOCAL), BF16),
            v((2, HALF, LOCAL), BF16),
            v((4, WIDTH, WIDTH), F32),
            v((2, 1024, LOCAL), F32),
            v((2, 512, LOCAL), F32),
            v((2, 512, LOCAL), F32),
            v((512, LOCAL), F32),
            v((512, LOCAL), F32),
            v((16, 32, LOCAL), F32),
            v((32, LOCAL), F32),
            v((4, 8, LOCAL), F32),
            v((8, LOCAL), F32),
            v((32, LOCAL), F32),
            v((512, LOCAL), F32),
            sems(1), sems(BALLS), sems(BALLS), sems(BALLS), sems(BALLS), sems(32),
            sems(1), sems(1), sems(16), sems(4), sems(4), sems(16), sems(1),
        ],
        compiler_params=pltpu.CompilerParams(
            collective_id=0, has_side_effects=True, vmem_limit_bytes=56 * 1024 * 1024
        ),
        cost_estimate=pl.CostEstimate(flops=8 * 10**9, bytes_accessed=8 * 10**6, transcendentals=4 * 10**6),
    )(gathered, cot, small, slots, w, wo)


def local(points, order, norm_gain, qkv_weight, out_weight, tree_gain, partner_slot, cotangent):
    gathered = permute_rows(gather_kernel, order, points)
    small = jnp.concatenate([norm_gain[None], tree_gain, jnp.zeros((3, LOCAL), F32)], axis=0)
    slots = jnp.pad(partner_slot.astype(F32), ((0, 0), (0, LOCAL - LEVELS)))
    mixed, grads, total = run_main(gathered, cotangent, small, slots, qkv_weight, out_weight)
    point_grad = permute_rows(scatter_kernel, order, grads)
    qkv_total = total[:768].reshape(3, WIDTH, LOCAL)
    out_total = jnp.concatenate([total[768:896], total[896:]], axis=1)
    return (mixed, point_grad, qkv_total, out_total)


def solution(mesh):
    in_specs = (
        P("pts", "ch"),
        P("pts"),
        P("ch"),
        P(),
        P(),
        P(None, "ch"),
        P("pts", None),
        P("pts", "ch"),
    )
    out_specs = (P("pts", "ch"), P("pts", "ch"), P(None, None, "ch"), P("ch", None))
    return jax.shard_map(local, mesh=mesh, in_specs=in_specs, out_specs=out_specs, check_vma=False)
```

```python
import math

import jax
import jax.numpy as jnp
from jax import lax
from jax.experimental import pallas as pl
from jax.experimental.pallas import tpu as pltpu
from jax.sharding import PartitionSpec as P

HEAD = 32
BALL = 256
LEVELS = 4
EPSILON = 1e-06

ROWS = 4096
HALF = 2048
LOCAL = 128
WIDTH = 256
HEADS = 8
BALLS = 8
GROUP = 16
EARLY_COT = 4

F32 = jnp.float32
BF16 = jnp.bfloat16
MESH = pl.DeviceIdType.MESH
SCALE = HEAD ** (-0.5)
SCALE_LOG2 = SCALE * math.log2(math.e)


def nn(left, right):
    return lax.dot_general(left, right, (((1,), (0,)), ((), ())), preferred_element_type=F32)


def nt(left, right):
    return lax.dot_general(left, right, (((1,), (1,)), ((), ())), preferred_element_type=F32)


def scatter_kernel(order_ref, rows_ref, out_ref, wide, moved):
    wide[...] = rows_ref[...].astype(F32)

    def step(block, carry):
        base = block * 16
        for inner in range(16):
            row = order_ref[base + inner]
            moved[pl.ds(row, 1), :] = wide[pl.ds(base + inner, 1), :]
        return carry

    lax.fori_loop(0, ROWS // 16, step, 0)
    out_ref[...] = moved[...].astype(BF16)


def permute_rows(kernel, order, rows):
    return pl.pallas_call(
        kernel,
        out_shape=jax.ShapeDtypeStruct((ROWS, LOCAL), BF16),
        in_specs=[pl.BlockSpec(memory_space=pltpu.SMEM), pl.BlockSpec(memory_space=pltpu.VMEM)],
        out_specs=pl.BlockSpec(memory_space=pltpu.VMEM),
        scratch_shapes=[pltpu.VMEM((ROWS, LOCAL), F32), pltpu.VMEM((ROWS, LOCAL), F32)],
        compiler_params=pltpu.CompilerParams(vmem_limit_bytes=24 * 1024 * 1024),
    )(order, rows)


def exact_dot(onehot, values):
    high = values.astype(BF16)
    rest = values - high.astype(F32)
    middle = rest.astype(BF16)
    low = (rest - middle.astype(F32)).astype(BF16)
    parts = nn(onehot, jnp.concatenate([high, middle, low], axis=1))
    return parts[:, :LOCAL] + parts[:, LOCAL:2 * LOCAL] + parts[:, 2 * LOCAL:]


def main_kernel(
    order_ref, points, cot, gain_ref, tree_gain_ref, slots, w, wo,
    mixed, grads, qkv_out, out_out,
    wide, moved, theirs_rows, xh, cth, sm, wt, wcat, vn, q_t, k_t, att_t, nrm, hid, inv, probs,
    early, nodes_own, nodes, picks, picks_t, final_state, final_grad, node_grads,
    pstage, precv, gstage, acc_t,
    acc, recv_a, sum_a, recv_c, sum_c, recv_z, all_f, total,
    s_small, s_pts, s_cot, s_proj, s_grad, s_early, s_tree, s_ng, s_a, s_c, s_z, s_f, s_g,
):
    p = lax.axis_index("pts")
    c = lax.axis_index("ch")
    core = p % 2
    plane = (p // 2) % 16
    depth = p // 32
    other_c = 1 - c
    local_range = p % GROUP
    me = local_range * 2 + c
    group_base = (p // GROUP) * GROUP
    ring = depth * 2 + c
    pair = (p, other_c)
    sibling = (p + 1 - 2 * core, c)

    def tree_peer(distance):
        there = (me + distance) % 32
        return (group_base + there // 2, there % 2)

    def early_peer(distance):
        return (group_base + (local_range + distance) % GROUP, c)

    def plane_index(distance):
        return (plane + distance) % 16

    def plane_peer(distance):
        return (depth * 32 + plane_index(distance) * 2 + core, c)

    def ring_peer(distance):
        there = (ring + distance) % 8
        return ((there // 2) * 32 + plane * 2 + core, there % 2)

    barrier = pltpu.get_barrier_semaphore()

    def greet(target):
        pl.semaphore_signal(barrier, inc=1, device_id=target, device_id_type=MESH)

    for distance in range(1, 32):
        greet(tree_peer(distance))
    far_base = (1 - plane // 8) * 8
    for step in range(8):
        greet((depth * 32 + (far_base + step) * 2 + core, c))
    for step in range(1, 4):
        for half in range(2):
            greet((((depth + step) % 4) * 32 + plane * 2 + core, half))

    def send(src, dst, sems, index, target):
        return pltpu.make_async_remote_copy(
            src_ref=src, dst_ref=dst, send_sem=sems.at[0, index], recv_sem=sems.at[1, index],
            device_id=target, device_id_type=MESH,
        )

    def theirs(ball):
        return pl.ds(pl.multiple_of(other_c * HALF + ball * BALL, BALL), BALL)

    def ours(ball):
        return pl.ds(pl.multiple_of(c * HALF + ball * BALL, BALL), BALL)

    def here(ball):
        return pl.ds(pl.multiple_of(ball * BALL, BALL), BALL)

    def small_copy():
        return send(sm.at[c], sm.at[c], s_small, 0, pair)

    def points_copy(ball):
        return send(theirs_rows.at[here(ball)], xh.at[c, here(ball)], s_pts, ball, pair)

    def cot_copy(ball):
        return send(cot.at[theirs(ball)], cth.at[c, here(ball)], s_cot, ball, pair)

    def proj_copy(ball):
        return send(pstage.at[other_c, here(ball)], precv.at[here(ball)], s_proj, ball, pair)

    def grad_copy(ball):
        return send(gstage.at[other_c, here(ball)], grads.at[ours(ball)], s_grad, ball, pair)

    def both(ref, rows):
        return jnp.concatenate([ref[0, rows, :], ref[1, rows, :]], axis=1).astype(F32)

    wide[...] = points[...].astype(F32)

    def pick_rows(start):
        def step(block, carry):
            base = start + block * 16
            for inner in range(16):
                row = order_ref[base + inner]
                moved[pl.ds(base + inner, 1), :] = wide[pl.ds(row, 1), :]
            return carry

        lax.fori_loop(0, BALL // 16, step, 0)
        return moved[pl.ds(pl.multiple_of(start, BALL), BALL), :].astype(BF16)

    def their_ball(ball, carry):
        theirs_rows[here(ball), :] = pick_rows(other_c * HALF + ball * BALL)
        points_copy(ball).start()
        return carry

    theirs_rows[0:BALL, :] = pick_rows(other_c * HALF)
    own_small = jnp.concatenate([gain_ref[...], tree_gain_ref[...], jnp.zeros((3, LOCAL), F32)], axis=0)
    sm[pl.ds(c, 1)] = own_small[None]
    pl.semaphore_wait(barrier, 45)
    small_copy().start()
    points_copy(0).start()
    lax.fori_loop(1, BALLS, their_ball, 0)

    early_rows = pl.ds(pl.multiple_of(local_range * 16, 16), 16)
    sums = [
        jnp.sum(cot[ball * BALL:(ball + 1) * BALL, :].astype(F32), axis=0, keepdims=True)
        for ball in range(ROWS // BALL)
    ]
    early[early_rows, 0:LOCAL] = jnp.concatenate(sums, axis=0)
    early[early_rows, LOCAL:] = jnp.concatenate(
        [slots[...].astype(F32), jnp.zeros((16, LOCAL - LEVELS), F32)], axis=1
    )

    def early_copy(distance):
        block = early.at[early_rows]
        return send(block, block, s_early, distance, early_peer(distance))

    for distance in range(1, GROUP):
        early_copy(distance).start()

    cth[pl.ds(c, 1)] = cot[pl.ds(pl.multiple_of(c * HALF, HALF), HALF), :][None]
    for index in range(3):
        wt[index] = jnp.transpose(w[index])
        wcat[:, index * WIDTH:(index + 1) * WIDTH] = w[index]

    def own_ball(ball, carry):
        xh[pl.ds(c, 1), here(ball), :] = pick_rows(c * HALF + ball * BALL)[None]
        return carry

    lax.fori_loop(0, BALLS, own_ball, 0)
    small_copy().wait_recv()
    gain = jnp.concatenate([sm[0, 0:1, :], sm[1, 0:1, :]], axis=1)
    bands = [slice(head * HEAD, (head + 1) * HEAD) for head in range(HEADS)]

    def forward(ball, carry):
        rows = here(ball)
        points_copy(ball).wait_recv()

        @pl.when(ball < EARLY_COT)
        def _():
            cot_copy(ball).start()

        ordered = both(xh, rows)
        mean = jnp.sum(ordered * ordered, axis=1, keepdims=True) * (1.0 / WIDTH)
        inverse = lax.rsqrt(mean + EPSILON)
        normed = (ordered * inverse * gain).astype(BF16)
        keyset = nn(normed, w[1]).astype(BF16)
        query_t = nt(wt[0], normed).astype(BF16)
        value_t = nt(wt[2], normed).astype(BF16)
        scores = [nn(keyset[:, band], query_t[band, :]) for band in bands]
        key_t = nt(wt[1], normed).astype(BF16)
        value = nn(normed, w[2]).astype(BF16)
        halves = []
        for head in range(HEADS):
            top = jnp.max(scores[head], axis=0, keepdims=True)
            weights = jnp.exp2((scores[head] - top) * SCALE_LOG2)
            scaled = weights * (1.0 / jnp.sum(weights, axis=0, keepdims=True))
            probs[ball * HEADS + head] = scaled
            halves.append(scaled.astype(BF16))
        attended_t = jnp.concatenate(
            [nn(value_t[band, :], half).astype(BF16) for band, half in zip(bands, halves)], axis=0
        )
        projected = nn(jnp.transpose(attended_t), wo[...])
        hidden = ordered + projected
        node = jnp.sum(hidden, axis=0, keepdims=True) * BALL ** (-0.5)
        nodes_own[0, pl.ds(ball, 1), :] = node[:, :LOCAL]
        nodes_own[1, pl.ds(ball, 1), :] = node[:, LOCAL:]
        hid[0, rows, :] = hidden[:, :LOCAL]
        hid[1, rows, :] = hidden[:, LOCAL:]
        pstage[0, rows, :] = projected[:, :LOCAL].astype(BF16)
        pstage[1, rows, :] = projected[:, LOCAL:].astype(BF16)
        inv[rows, :] = jnp.broadcast_to(inverse, (BALL, LOCAL))
        nrm[rows, :] = normed
        vn[rows, :] = value
        q_t[ball] = query_t
        k_t[ball] = key_t
        att_t[ball] = attended_t
        return carry

    lax.fori_loop(0, BALLS, forward, 0)

    node_rows = pl.ds(pl.multiple_of(me * BALLS, BALLS), BALLS)

    def tree_copy(distance):
        return send(
            nodes_own.at[(me + distance) % 2], nodes.at[node_rows], s_tree, distance, tree_peer(distance)
        )

    for distance in range(1, 32):
        tree_copy(distance).start()
    for ball in range(EARLY_COT, BALLS):
        cot_copy(ball).start()
    nodes[node_rows, :] = nodes_own[pl.ds(c, 1)][0]

    for distance in range(1, GROUP):
        early_copy(distance).wait_recv()
    count = GROUP * 16
    range_ids = lax.broadcasted_iota(jnp.int32, (count, 1), 0) // 16
    lane_ids = lax.broadcasted_iota(jnp.int32, (count, count), 1)
    for level in range(LEVELS):
        slot = early[:, LOCAL + level:LOCAL + level + 1].astype(jnp.int32)
        bit = (range_ids // (1 << level)) % 2
        partner = (range_ids + (1 - 2 * bit) * (1 << level)) * 16 + slot
        onehot = jnp.where(lane_ids == partner, 1.0, 0.0).astype(BF16)
        picks[level] = onehot
        picks_t[level] = jnp.transpose(onehot)
    acc_t[...] = jnp.zeros_like(acc_t)
    own_gains = sm[pl.ds(c, 1)][0]

    for distance in range(1, 32):
        tree_copy(distance).wait_recv()
    states = nodes[...]
    chosen_list = []
    for level in range(LEVELS):
        chosen = exact_dot(picks[level], states)
        states = states + own_gains[1 + level:2 + level, :] * (chosen * jax.nn.sigmoid(chosen))
        chosen_list.append(chosen)
    node_grad = early[:, 0:LOCAL]
    for level in reversed(range(LEVELS)):
        chosen = chosen_list[level]
        sigma = jax.nn.sigmoid(chosen)
        slope = sigma * (1.0 + chosen * (1.0 - sigma))
        node_grad = node_grad + exact_dot(
            picks_t[level], own_gains[1 + level:2 + level, :] * slope * node_grad
        )
    final_grad[...] = node_grad
    final_state[...] = states

    def range_row(half, ball):
        return local_range * 16 + half * BALLS + ball

    def ng_copy():
        part = final_grad.at[pl.ds(pl.multiple_of(range_row(other_c, 0), BALLS), BALLS)]
        return send(part, node_grads.at[c], s_ng, 0, pair)

    ng_copy().start()
    for ball in range(BALLS):
        proj_copy(ball).start()
    node_grads[pl.ds(c, 1)] = final_grad[pl.ds(pl.multiple_of(range_row(c, 0), BALLS), BALLS), :][None]

    def own_mixed(ball, carry):
        state = final_state[pl.ds(range_row(c, ball), 1), :]
        mixed[ours(ball), :] = (hid[pl.ds(c, 1), here(ball), :][0] + state).astype(BF16)
        return carry

    lax.fori_loop(0, BALLS, own_mixed, 0)
    ng_copy().wait_recv()

    def backward(ball, carry):
        rows = here(ball)
        cot_copy(ball).wait_recv()
        shift = jnp.concatenate(
            [node_grads[0, pl.ds(ball, 1), :], node_grads[1, pl.ds(ball, 1), :]], axis=1
        ) * BALL ** (-0.5)
        hidden_grad = (both(cth, rows) + shift).astype(BF16)
        att_grad = nt(wo[...], hidden_grad).astype(BF16)
        value = vn[rows, :]
        prob_grads = [nn(value[:, band], att_grad[band, :]) for band in bands]
        acc_t[768:1024, :] += nn(att_t[ball], hidden_grad)
        score_grads, halves = [], []
        for head in range(HEADS):
            prob = probs[ball * HEADS + head]
            dots = jnp.sum(prob_grads[head] * prob, axis=0, keepdims=True)
            score_grads.append((prob * (prob_grads[head] - dots) * SCALE).astype(BF16))
            halves.append(prob.astype(BF16))
        dv = [nt(att_grad[band, :], half).astype(BF16) for band, half in zip(bands, halves)]
        key_t = k_t[ball]
        dq = [nn(key_t[band, :], part).astype(BF16) for band, part in zip(bands, score_grads)]
        query_t = q_t[ball]
        dk = [nt(query_t[band, :], part).astype(BF16) for band, part in zip(bands, score_grads)]
        all_grads = jnp.concatenate(dq + dk + dv, axis=0)
        normed_grad = nn(wcat[...], all_grads)
        acc_t[0:768, :] += nn(all_grads, nrm[rows, :])
        scaled_grad = jnp.transpose(normed_grad) * gain
        ordered = both(xh, rows)
        inverse = jnp.concatenate([inv[rows, :], inv[rows, :]], axis=1)
        correction = jnp.sum(ordered * scaled_grad, axis=1, keepdims=True) * (1.0 / WIDTH)
        ordered_grad = (
            hidden_grad.astype(F32) + inverse * scaled_grad - ordered * (inverse * inverse * inverse) * correction
        ).astype(BF16)
        gstage[0, rows, :] = ordered_grad[:, :LOCAL]
        gstage[1, rows, :] = ordered_grad[:, LOCAL:]
        grad_copy(ball).start()
        grads[ours(ball), :] = gstage[pl.ds(c, 1), rows, :][0]
        return carry

    lax.fori_loop(0, BALLS, backward, 0)

    for index in range(3):
        part = jnp.transpose(acc_t[index * 256:(index + 1) * 256, :])
        acc[0, index * 256:(index + 1) * 256, :] = part[:, :LOCAL]
        acc[1, index * 256:(index + 1) * 256, :] = part[:, LOCAL:]
    for half in range(2):
        band = slice(768 + half * LOCAL, 768 + (half + 1) * LOCAL)
        acc[half, 768:896, :] = acc_t[band, :LOCAL]
        acc[half, 896:1024, :] = acc_t[band, LOCAL:]

    kept = pl.ds(pl.multiple_of(core * 512, 512), 512)
    given = pl.ds(pl.multiple_of((1 - core) * 512, 512), 512)
    copy_a = send(acc.at[:, given], recv_a, s_a, 0, sibling)
    copy_a.start()

    def their_mixed(ball, carry):
        rows = here(ball)
        proj_copy(ball).wait_recv()
        state = final_state[pl.ds(range_row(other_c, ball), 1), :]
        mixed[theirs(ball), :] = (
            theirs_rows[rows, :].astype(F32) + precv[rows, :].astype(F32) + state
        ).astype(BF16)
        return carry

    copy_a.wait_recv()
    sum_a[...] = acc[:, kept, :] + recv_a[...]

    def copy_c(distance):
        piece = pl.ds(pl.multiple_of(plane_index(distance) * 32, 32), 32)
        return send(sum_a.at[:, piece], recv_c.at[distance], s_c, distance, plane_peer(distance))

    for distance in range(1, 16):
        copy_c(distance).start()
    lax.fori_loop(0, BALLS, their_mixed, 0)
    part = sum_a[:, pl.ds(pl.multiple_of(plane * 32, 32), 32), :]
    for distance in range(1, 16):
        copy_c(distance).wait_recv()
        part = part + recv_c[distance]
    sum_c[...] = part

    def copy_z(distance):
        return send(sum_c.at[(ring + distance) % 2], recv_z.at[ring], s_z, distance, ring_peer(distance))

    for distance in range(1, 8):
        copy_z(distance).start()
    recv_z[pl.ds(ring, 1)] = sum_c[pl.ds(c, 1)]
    for distance in range(1, 8):
        copy_z(distance).wait_recv()
    part = recv_z[0]
    for step in range(1, 8):
        part = part + recv_z[step]
    plane_rows = pl.ds(pl.multiple_of(plane * 32, 32), 32)
    all_f[plane_rows, :] = part

    def copy_f(distance):
        return send(all_f.at[plane_rows], all_f.at[plane_rows], s_f, distance, plane_peer(distance))

    for distance in range(1, 16):
        copy_f(distance).start()
    for distance in range(1, 16):
        copy_f(distance).wait_recv()

    copy_g = send(all_f, total.at[kept], s_g, 0, sibling)
    copy_g.start()
    total[kept, :] = all_f[...]
    copy_g.wait_recv()
    for index in range(3):
        qkv_out[index] = total[index * 256:(index + 1) * 256, :]
    out_out[:, :LOCAL] = total[768:896, :]
    out_out[:, LOCAL:] = total[896:1024, :]

    small_copy().wait_send()
    ng_copy().wait_send()

    def settle(ball, carry):
        points_copy(ball).wait_send()
        cot_copy(ball).wait_send()
        proj_copy(ball).wait_send()
        grad_copy(ball).wait()
        return carry

    lax.fori_loop(0, BALLS, settle, 0)
    for distance in range(1, 32):
        tree_copy(distance).wait_send()
    copy_a.wait_send()
    for distance in range(1, 16):
        early_copy(distance).wait_send()
        copy_c(distance).wait_send()
        copy_f(distance).wait_send()
    for distance in range(1, 8):
        copy_z(distance).wait_send()
    copy_g.wait_send()


def run_main(order, points, cot, gain, tree_gain, slots, w, wo):
    vmem = pl.BlockSpec(memory_space=pltpu.VMEM)
    sems = lambda count: pltpu.SemaphoreType.DMA((2, count))
    v = pltpu.VMEM
    return pl.pallas_call(
        main_kernel,
        out_shape=(
            jax.ShapeDtypeStruct((ROWS, LOCAL), BF16),
            jax.ShapeDtypeStruct((ROWS, LOCAL), BF16),
            jax.ShapeDtypeStruct((3, WIDTH, LOCAL), F32),
            jax.ShapeDtypeStruct((LOCAL, WIDTH), F32),
        ),
        in_specs=[pl.BlockSpec(memory_space=pltpu.SMEM)] + [vmem] * 7,
        out_specs=(vmem,) * 4,
        scratch_shapes=[
            v((ROWS, LOCAL), F32),
            v((ROWS, LOCAL), F32),
            v((HALF, LOCAL), BF16),
            v((2, HALF, LOCAL), BF16),
            v((2, HALF, LOCAL), BF16),
            v((2, 8, LOCAL), F32),
            v((3, WIDTH, WIDTH), BF16),
            v((WIDTH, 3 * WIDTH), BF16),
            v((HALF, WIDTH), BF16),
            v((BALLS, WIDTH, BALL), BF16),
            v((BALLS, WIDTH, BALL), BF16),
            v((BALLS, WIDTH, BALL), BF16),
            v((HALF, WIDTH), BF16),
            v((2, HALF, LOCAL), F32),
            v((HALF, LOCAL), F32),
            v((BALLS * HEADS, BALL, BALL), F32),
            v((256, 2 * LOCAL), F32),
            v((2, BALLS, LOCAL), F32),
            v((256, LOCAL), F32),
            v((LEVELS, 256, 256), BF16),
            v((LEVELS, 256, 256), BF16),
            v((256, LOCAL), F32),
            v((256, LOCAL), F32),
            v((2, BALLS, LOCAL), F32),
            v((2, HALF, LOCAL), BF16),
            v((HALF, LOCAL), BF16),
            v((2, HALF, LOCAL), BF16),
            v((1024, WIDTH), F32),
            v((2, 1024, LOCAL), F32),
            v((2, 512, LOCAL), F32),
            v((2, 512, LOCAL), F32),
            v((16, 2, 32, LOCAL), F32),
            v((2, 32, LOCAL), F32),
            v((8, 32, LOCAL), F32),
            v((512, LOCAL), F32),
            v((1024, LOCAL), F32),
            sems(1), sems(BALLS), sems(BALLS), sems(BALLS), sems(BALLS), sems(16), sems(32),
            sems(1), sems(1), sems(16), sems(8), sems(16), sems(1),
        ],
        compiler_params=pltpu.CompilerParams(
            collective_id=0, has_side_effects=True, vmem_limit_bytes=58 * 1024 * 1024
        ),
        cost_estimate=pl.CostEstimate(flops=8 * 10**9, bytes_accessed=8 * 10**6, transcendentals=4 * 10**6),
    )(order, points, cot, gain, tree_gain, slots, w, wo)


def local(points, order, norm_gain, qkv_weight, out_weight, tree_gain, partner_slot, cotangent):
    mixed, grads, qkv_total, out_total = run_main(
        order, points, cotangent, norm_gain[None], tree_gain, partner_slot, qkv_weight, out_weight
    )
    point_grad = permute_rows(scatter_kernel, order, grads)
    return (mixed, point_grad, qkv_total, out_total)


def solution(mesh):
    in_specs = (
        P("pts", "ch"),
        P("pts"),
        P("ch"),
        P(),
        P(),
        P(None, "ch"),
        P("pts", None),
        P("pts", "ch"),
    )
    out_specs = (P("pts", "ch"), P("pts", "ch"), P(None, None, "ch"), P("ch", None))
    return jax.shard_map(local, mesh=mesh, in_specs=in_specs, out_specs=out_specs, check_vma=False)
```

```python
import math

import jax
import jax.numpy as jnp
from jax import lax
from jax.experimental import pallas as pl
from jax.experimental.pallas import tpu as pltpu
from jax.sharding import PartitionSpec as P

HEAD = 32
BALL = 256
LEVELS = 4
EPSILON = 1e-06

ROWS = 4096
HALF = 2048
LOCAL = 128
WIDTH = 256
HEADS = 8
BALLS = 8
GROUP = 16
EARLY_COT = 4

F32 = jnp.float32
BF16 = jnp.bfloat16
MESH = pl.DeviceIdType.MESH
SCALE = HEAD ** (-0.5)
SCALE_LOG2 = SCALE * math.log2(math.e)


def nn(left, right):
    return lax.dot_general(left, right, (((1,), (0,)), ((), ())), preferred_element_type=F32)


def nt(left, right):
    return lax.dot_general(left, right, (((1,), (1,)), ((), ())), preferred_element_type=F32)


def exact_dot(onehot, values):
    high = values.astype(BF16)
    rest = values - high.astype(F32)
    middle = rest.astype(BF16)
    low = (rest - middle.astype(F32)).astype(BF16)
    parts = nn(onehot, jnp.concatenate([high, middle, low], axis=1))
    return parts[:, :LOCAL] + parts[:, LOCAL:2 * LOCAL] + parts[:, 2 * LOCAL:]


def main_kernel(
    order_ref, order_rows, points, cot, gain_ref, tree_gain_ref, slots_t, w, wo,
    mixed, point_grad, qkv_out, out_out,
    wide, moved, theirs_rows, xh, cth, sm, wt, wcat, vn, q_t, k_t, att_t, nrm, hid, inv, probs,
    early, chip_nodes, nodes, picks, picks_t, final_state, final_grad, node_grads,
    pstage, precv, gstage, acc_t,
    acc, recv_a, sum_a, half_a, recv_c, sum_c, recv_z, all_f, total,
    grads, places, places_smem, s_places,
    s_small, s_pts, s_cot, s_proj, s_grad, s_early, s_tree, s_ng, s_a, s_c, s_z, s_f, s_g,
):
    p = lax.axis_index("pts")
    c = lax.axis_index("ch")
    core = p % 2
    plane = (p // 2) % 16
    depth = p // 32
    other_c = 1 - c
    local_range = p % GROUP
    chip = local_range // 2
    group_base = (p // GROUP) * GROUP
    ring = depth * 2 + c
    pair = (p, other_c)
    sibling = (p + 1 - 2 * core, c)

    def tree_peer(distance):
        there = (chip * 2 + c + distance) % 16
        return (group_base + (there // 2) * 2 + core, there % 2)

    def early_peer(distance):
        return (group_base + ((chip + distance) % 8) * 2 + core, c)

    def plane_index(distance):
        return (plane + distance) % 16

    def plane_peer(distance):
        return (depth * 32 + plane_index(distance) * 2 + core, c)

    def ring_peer(distance):
        there = (ring + distance) % 8
        return ((there // 2) * 32 + plane * 2 + core, there % 2)

    barrier = pltpu.get_barrier_semaphore()

    def greet(target):
        pl.semaphore_signal(barrier, inc=1, device_id=target, device_id_type=MESH)

    greet(sibling)
    for distance in range(1, 16):
        greet(tree_peer(distance))
    far_base = (1 - plane // 8) * 8
    for step in range(8):
        greet((depth * 32 + (far_base + step) * 2 + core, c))
    for step in range(1, 4):
        for half in range(2):
            greet((((depth + step) % 4) * 32 + plane * 2 + core, half))

    def send(src, dst, sems, index, target):
        return pltpu.make_async_remote_copy(
            src_ref=src, dst_ref=dst, send_sem=sems.at[0, index], recv_sem=sems.at[1, index],
            device_id=target, device_id_type=MESH,
        )

    def theirs(ball):
        return pl.ds(pl.multiple_of(other_c * HALF + ball * BALL, BALL), BALL)

    def ours(ball):
        return pl.ds(pl.multiple_of(c * HALF + ball * BALL, BALL), BALL)

    def here(ball):
        return pl.ds(pl.multiple_of(ball * BALL, BALL), BALL)

    def small_copy():
        return send(sm.at[c], sm.at[c], s_small, 0, pair)

    def points_copy(ball):
        return send(theirs_rows.at[here(ball)], xh.at[c, here(ball)], s_pts, ball, pair)

    def cot_copy(ball):
        return send(cot.at[theirs(ball)], cth.at[c, here(ball)], s_cot, ball, pair)

    def proj_copy(ball):
        return send(pstage.at[other_c, here(ball)], precv.at[here(ball)], s_proj, ball, pair)

    def grad_copy(ball):
        return send(gstage.at[other_c, here(ball)], grads.at[ours(ball)], s_grad, ball, pair)

    def both(ref, rows):
        return jnp.concatenate([ref[0, rows, :], ref[1, rows, :]], axis=1).astype(F32)

    wide[...] = points[...].astype(F32)

    def pick_rows(start):
        def step(block, carry):
            base = start + block * 16
            for inner in range(16):
                row = order_ref[base + inner]
                moved[pl.ds(base + inner, 1), :] = wide[pl.ds(row, 1), :]
            return carry

        lax.fori_loop(0, BALL // 16, step, 0)
        return moved[pl.ds(pl.multiple_of(start, BALL), BALL), :].astype(BF16)

    def their_ball(ball, carry):
        theirs_rows[here(ball), :] = pick_rows(other_c * HALF + ball * BALL)
        points_copy(ball).start()
        return carry

    theirs_rows[0:BALL, :] = pick_rows(other_c * HALF)
    own_small = jnp.concatenate([gain_ref[...], tree_gain_ref[...], jnp.zeros((3, LOCAL), F32)], axis=0)
    sm[pl.ds(c, 1)] = own_small[None]
    pl.semaphore_wait(barrier, 30)
    small_copy().start()
    points_copy(0).start()
    lax.fori_loop(1, BALLS, their_ball, 0)

    slots = jnp.transpose(
        jnp.concatenate(
            [
                jnp.concatenate([slots_t[...].astype(F32), jnp.zeros((LEVELS, LOCAL - 16), F32)], axis=1),
                jnp.zeros((LOCAL - LEVELS, LOCAL), F32),
            ],
            axis=0,
        )
    )
    range_rows = pl.ds(pl.multiple_of(local_range * BALLS, BALLS), BALLS)
    chip_rows = pl.ds(pl.multiple_of(chip * 16, 16), 16)
    for half in range(2):
        sums = [
            jnp.sum(cot[ball * BALL:(ball + 1) * BALL, :].astype(F32), axis=0, keepdims=True)
            for ball in range(half * BALLS, (half + 1) * BALLS)
        ]
        early[half, range_rows, 0:LOCAL] = jnp.concatenate(sums, axis=0)
        early[half, range_rows, LOCAL:] = slots[half * BALLS:(half + 1) * BALLS, :]

    def early_first():
        block = early.at[:, range_rows]
        return send(block, block, s_early, 0, sibling)

    def early_copy(distance):
        block = early.at[:, chip_rows]
        return send(block, block, s_early, distance, early_peer(distance))

    early_first().start()

    cth[pl.ds(c, 1)] = cot[pl.ds(pl.multiple_of(c * HALF, HALF), HALF), :][None]
    for index in range(3):
        wt[index] = jnp.transpose(w[index])
        wcat[:, index * WIDTH:(index + 1) * WIDTH] = w[index]

    def own_ball(ball, carry):
        xh[pl.ds(c, 1), here(ball), :] = pick_rows(c * HALF + ball * BALL)[None]
        return carry

    lax.fori_loop(0, BALLS, own_ball, 0)
    early_first().wait_recv()
    for distance in range(1, 8):
        early_copy(distance).start()
    small_copy().wait_recv()
    gain = jnp.concatenate([sm[0, 0:1, :], sm[1, 0:1, :]], axis=1)
    bands = [slice(head * HEAD, (head + 1) * HEAD) for head in range(HEADS)]

    def two(step):
        return pl.ds(pl.multiple_of(step * 2 * BALL, 2 * BALL), 2 * BALL)

    pieces = [(side, band) for side in range(2) for band in bands]
    sides = [slice(0, BALL), slice(BALL, 2 * BALL)]

    def forward(step, carry):
        rows = two(step)
        for side in range(2):
            points_copy(2 * step + side).wait_recv()

        @pl.when(step < EARLY_COT // 2)
        def _():
            for side in range(2):
                cot_copy(2 * step + side).start()

        ordered = both(xh, rows)
        mean = jnp.sum(ordered * ordered, axis=1, keepdims=True) * (1.0 / WIDTH)
        inverse = lax.rsqrt(mean + EPSILON)
        normed = (ordered * inverse * gain).astype(BF16)
        keyset = nn(normed, w[1]).astype(BF16)
        query_t = nt(wt[0], normed).astype(BF16)
        value_t = nt(wt[2], normed).astype(BF16)
        scores = [nn(keyset[sides[side], band], query_t[band, sides[side]]) for side, band in pieces]
        key_t = nt(wt[1], normed).astype(BF16)
        value = nn(normed, w[2]).astype(BF16)
        halves = []
        for index in range(2 * HEADS):
            top = jnp.max(scores[index], axis=0, keepdims=True)
            weights = jnp.exp2((scores[index] - top) * SCALE_LOG2)
            scaled = weights * (1.0 / jnp.sum(weights, axis=0, keepdims=True))
            probs[step * 2 * HEADS + index] = scaled
            halves.append(scaled.astype(BF16))
        parts = [
            nn(value_t[band, sides[side]], half).astype(BF16) for (side, band), half in zip(pieces, halves)
        ]
        attended_t = jnp.concatenate(
            [jnp.concatenate(parts[:HEADS], axis=0), jnp.concatenate(parts[HEADS:], axis=0)], axis=1
        )
        projected = nn(jnp.transpose(attended_t), wo[...])
        hidden = ordered + projected
        for side in range(2):
            node = jnp.sum(hidden[sides[side], :], axis=0, keepdims=True) * BALL ** (-0.5)
            row = pl.ds(core * BALLS + 2 * step + side, 1)
            chip_nodes[0, row, :] = node[:, :LOCAL]
            chip_nodes[1, row, :] = node[:, LOCAL:]
            q_t[2 * step + side] = query_t[:, sides[side]]
            k_t[2 * step + side] = key_t[:, sides[side]]
        hid[0, rows, :] = hidden[:, :LOCAL]
        hid[1, rows, :] = hidden[:, LOCAL:]
        pstage[0, rows, :] = projected[:, :LOCAL].astype(BF16)
        pstage[1, rows, :] = projected[:, LOCAL:].astype(BF16)
        inv[rows, :] = jnp.broadcast_to(inverse, (2 * BALL, LOCAL))
        nrm[rows, :] = normed
        vn[rows, :] = value
        att_t[step] = attended_t
        return carry

    lax.fori_loop(0, BALLS // 2, forward, 0)

    core_rows = pl.ds(pl.multiple_of(core * BALLS, BALLS), BALLS)

    def tree_first():
        block = chip_nodes.at[:, core_rows]
        return send(block, block, s_tree, 0, sibling)

    def tree_copy(distance):
        return send(
            chip_nodes.at[(c + distance) % 2], nodes.at[c, chip_rows], s_tree, distance, tree_peer(distance)
        )

    tree_first().start()
    tree_first().wait_recv()
    for distance in range(1, 16):
        tree_copy(distance).start()
    for ball in range(EARLY_COT, BALLS):
        cot_copy(ball).start()
    nodes[pl.ds(c, 1), chip_rows, :] = chip_nodes[pl.ds(c, 1)]

    for distance in range(1, 8):
        early_copy(distance).wait_recv()
    count = GROUP * 16
    range_ids = (lax.broadcasted_iota(jnp.int32, (count, 1), 0) % LOCAL) // BALLS
    lane_ids = lax.broadcasted_iota(jnp.int32, (count, count), 1)
    known = jnp.concatenate([early[0], early[1]], axis=0)
    for level in range(LEVELS):
        slot = known[:, LOCAL + level:LOCAL + level + 1].astype(jnp.int32)
        bit = (range_ids // (1 << level)) % 2
        partner = (slot // BALLS) * LOCAL + (range_ids + (1 - 2 * bit) * (1 << level)) * BALLS + slot % BALLS
        onehot = jnp.where(lane_ids == partner, 1.0, 0.0).astype(BF16)
        picks[level] = onehot
        picks_t[level] = jnp.transpose(onehot)
    acc_t[...] = jnp.zeros_like(acc_t)
    own_gains = sm[pl.ds(c, 1)][0]

    for distance in range(1, 16):
        tree_copy(distance).wait_recv()
    states = jnp.concatenate([nodes[0], nodes[1]], axis=0)
    chosen_list = []
    for level in range(LEVELS):
        chosen = exact_dot(picks[level], states)
        states = states + own_gains[1 + level:2 + level, :] * (chosen * jax.nn.sigmoid(chosen))
        chosen_list.append(chosen)
    node_grad = known[:, 0:LOCAL]
    for level in reversed(range(LEVELS)):
        chosen = chosen_list[level]
        sigma = jax.nn.sigmoid(chosen)
        slope = sigma * (1.0 + chosen * (1.0 - sigma))
        node_grad = node_grad + exact_dot(
            picks_t[level], own_gains[1 + level:2 + level, :] * slope * node_grad
        )
    final_grad[...] = node_grad
    final_state[...] = states

    def range_row(half, ball):
        return half * LOCAL + local_range * BALLS + ball

    def ng_copy():
        part = final_grad.at[pl.ds(pl.multiple_of(range_row(other_c, 0), BALLS), BALLS)]
        return send(part, node_grads.at[c], s_ng, 0, pair)

    ng_copy().start()
    for ball in range(BALLS):
        proj_copy(ball).start()
    node_grads[pl.ds(c, 1)] = final_grad[pl.ds(pl.multiple_of(range_row(c, 0), BALLS), BALLS), :][None]

    def own_mixed(ball, carry):
        state = final_state[pl.ds(range_row(c, ball), 1), :]
        mixed[ours(ball), :] = (hid[pl.ds(c, 1), here(ball), :][0] + state).astype(BF16)
        return carry

    lax.fori_loop(0, BALLS, own_mixed, 0)
    ng_copy().wait_recv()

    def backward(step, carry):
        rows = two(step)
        shifts = []
        for side in range(2):
            cot_copy(2 * step + side).wait_recv()
            row = pl.ds(2 * step + side, 1)
            shift = jnp.concatenate([node_grads[0, row, :], node_grads[1, row, :]], axis=1) * BALL ** (-0.5)
            shifts.append(jnp.broadcast_to(shift, (BALL, WIDTH)))
        hidden_grad = (both(cth, rows) + jnp.concatenate(shifts, axis=0)).astype(BF16)
        att_grad = nt(wo[...], hidden_grad).astype(BF16)
        value = vn[rows, :]
        prob_grads = [nn(value[sides[side], band], att_grad[band, sides[side]]) for side, band in pieces]
        acc_t[768:1024, :] += nn(att_t[step], hidden_grad)
        score_grads, halves = [], []
        for index in range(2 * HEADS):
            prob = probs[step * 2 * HEADS + index]
            dots = jnp.sum(prob_grads[index] * prob, axis=0, keepdims=True)
            score_grads.append((prob * (prob_grads[index] - dots) * SCALE).astype(BF16))
            halves.append(prob.astype(BF16))
        dv = [
            nt(att_grad[band, sides[side]], half).astype(BF16) for (side, band), half in zip(pieces, halves)
        ]
        dq = [
            nn(k_t[2 * step + side, band, :], part).astype(BF16)
            for (side, band), part in zip(pieces, score_grads)
        ]
        dk = [
            nt(q_t[2 * step + side, band, :], part).astype(BF16)
            for (side, band), part in zip(pieces, score_grads)
        ]
        all_grads = jnp.concatenate(
            [
                jnp.concatenate(dq[:HEADS] + dk[:HEADS] + dv[:HEADS], axis=0),
                jnp.concatenate(dq[HEADS:] + dk[HEADS:] + dv[HEADS:], axis=0),
            ],
            axis=1,
        )
        normed_grad = nn(wcat[...], all_grads)
        acc_t[0:768, :] += nn(all_grads, nrm[rows, :])
        scaled_grad = jnp.transpose(normed_grad) * gain
        ordered = both(xh, rows)
        inverse = jnp.concatenate([inv[rows, :], inv[rows, :]], axis=1)
        correction = jnp.sum(ordered * scaled_grad, axis=1, keepdims=True) * (1.0 / WIDTH)
        ordered_grad = (
            hidden_grad.astype(F32) + inverse * scaled_grad - ordered * (inverse * inverse * inverse) * correction
        ).astype(BF16)
        gstage[0, rows, :] = ordered_grad[:, :LOCAL]
        gstage[1, rows, :] = ordered_grad[:, LOCAL:]
        for side in range(2):
            grad_copy(2 * step + side).start()
        own = pl.ds(pl.multiple_of(c * HALF + step * 2 * BALL, 2 * BALL), 2 * BALL)
        grads[own, :] = gstage[pl.ds(c, 1), rows, :][0]
        return carry

    lax.fori_loop(0, BALLS // 2, backward, 0)

    for index in range(3):
        part = jnp.transpose(acc_t[index * 256:(index + 1) * 256, :])
        acc[0, index * 256:(index + 1) * 256, :] = part[:, :LOCAL]
        acc[1, index * 256:(index + 1) * 256, :] = part[:, LOCAL:]
    for half in range(2):
        band = slice(768 + half * LOCAL, 768 + (half + 1) * LOCAL)
        acc[half, 768:896, :] = acc_t[band, :LOCAL]
        acc[half, 896:1024, :] = acc_t[band, LOCAL:]

    kept = pl.ds(pl.multiple_of(core * 512, 512), 512)
    given = pl.ds(pl.multiple_of((1 - core) * 512, 512), 512)
    copy_a = send(acc.at[:, given], recv_a, s_a, 0, sibling)
    copy_a.start()

    tiles = ROWS // LOCAL
    lanes = lax.broadcasted_iota(jnp.int32, (1, LOCAL), 1)
    high_ids = lax.broadcasted_iota(jnp.int32, (tiles, LOCAL), 0)
    low_ids = lax.broadcasted_iota(jnp.int32, (LOCAL, LOCAL), 0)
    high_hits, low_hits = [], []
    for tile in range(tiles):
        target = order_rows[tile:tile + 1, :]
        high_hits.append(jnp.where(high_ids == target // LOCAL, 1.0, 0.0).astype(BF16))
        hit = low_ids == target % LOCAL
        source = lanes + tile * LOCAL
        low_hits.append(
            jnp.concatenate(
                [
                    jnp.where(hit, (source // 64).astype(F32), 0.0),
                    jnp.where(hit, (source % 64).astype(F32), 0.0),
                ],
                axis=0,
            ).astype(BF16)
        )
    found = nt(jnp.concatenate(high_hits, axis=1), jnp.concatenate(low_hits, axis=1))
    inverse_order = (found[:, :LOCAL] * 64.0 + found[:, LOCAL:]).astype(jnp.int32)
    places[...] = jnp.clip(inverse_order, 0, ROWS - 1)
    fetch = pltpu.make_async_copy(places, places_smem, s_places)
    fetch.start()

    def return_rows(start, stop):
        def step(block, carry):
            for inner in range(16):
                row = places_smem[block // 8, (block % 8) * 16 + inner]
                moved[pl.ds(block * 16 + inner, 1), :] = wide[pl.ds(row, 1), :]
            return carry

        lax.fori_loop(start // 16, stop // 16, step, 0)
        point_grad[start:stop, :] = moved[start:stop, :].astype(BF16)

    def their_mixed(ball, carry):
        rows = here(ball)
        proj_copy(ball).wait_recv()
        state = final_state[pl.ds(range_row(other_c, ball), 1), :]
        mixed[theirs(ball), :] = (
            theirs_rows[rows, :].astype(F32) + precv[rows, :].astype(F32) + state
        ).astype(BF16)
        return carry

    copy_a.wait_recv()
    sum_a[...] = acc[:, kept, :] + recv_a[...]
    half_a[...] = sum_a[...].astype(BF16)

    def copy_c(distance):
        piece = pl.ds(pl.multiple_of(plane_index(distance) * 32, 32), 32)
        return send(half_a.at[:, piece], recv_c.at[distance], s_c, distance, plane_peer(distance))

    for distance in range(1, 16):
        copy_c(distance).start()
    lax.fori_loop(0, BALLS, their_mixed, 0)
    for ball in range(BALLS):
        grad_copy(ball).wait_recv()
    wide[...] = grads[...].astype(F32)
    part = sum_a[:, pl.ds(pl.multiple_of(plane * 32, 32), 32), :]
    for distance in range(1, 16):
        copy_c(distance).wait_recv()
        part = part + recv_c[distance].astype(F32)
    sum_c[...] = part

    def copy_z(distance):
        return send(sum_c.at[(ring + distance) % 2], recv_z.at[ring], s_z, distance, ring_peer(distance))

    for distance in range(1, 8):
        copy_z(distance).start()
    recv_z[pl.ds(ring, 1)] = sum_c[pl.ds(c, 1)]
    fetch.wait()
    return_rows(0, HALF)
    for distance in range(1, 8):
        copy_z(distance).wait_recv()
    part = recv_z[0]
    for step in range(1, 8):
        part = part + recv_z[step]
    plane_rows = pl.ds(pl.multiple_of(plane * 32, 32), 32)
    all_f[plane_rows, :] = part

    def copy_f(distance):
        return send(all_f.at[plane_rows], all_f.at[plane_rows], s_f, distance, plane_peer(distance))

    for distance in range(1, 16):
        copy_f(distance).start()
    return_rows(HALF, ROWS)
    for distance in range(1, 16):
        copy_f(distance).wait_recv()

    copy_g = send(all_f, total.at[kept], s_g, 0, sibling)
    copy_g.start()
    total[kept, :] = all_f[...]
    copy_g.wait_recv()
    for index in range(3):
        qkv_out[index] = total[index * 256:(index + 1) * 256, :]
    out_out[:, :LOCAL] = total[768:896, :]
    out_out[:, LOCAL:] = total[896:1024, :]

    small_copy().wait_send()
    ng_copy().wait_send()

    def settle(ball, carry):
        points_copy(ball).wait_send()
        cot_copy(ball).wait_send()
        proj_copy(ball).wait_send()
        grad_copy(ball).wait_send()
        return carry

    lax.fori_loop(0, BALLS, settle, 0)
    tree_first().wait_send()
    early_first().wait_send()
    for distance in range(1, 8):
        early_copy(distance).wait_send()
    for distance in range(1, 16):
        tree_copy(distance).wait_send()
    copy_a.wait_send()
    for distance in range(1, 16):
        copy_c(distance).wait_send()
        copy_f(distance).wait_send()
    for distance in range(1, 8):
        copy_z(distance).wait_send()
    copy_g.wait_send()


def run_main(order, order_rows, points, cot, gain, tree_gain, slots, w, wo):
    vmem = pl.BlockSpec(memory_space=pltpu.VMEM)
    sems = lambda count: pltpu.SemaphoreType.DMA((2, count))
    v = pltpu.VMEM
    return pl.pallas_call(
        main_kernel,
        out_shape=(
            jax.ShapeDtypeStruct((ROWS, LOCAL), BF16),
            jax.ShapeDtypeStruct((ROWS, LOCAL), BF16),
            jax.ShapeDtypeStruct((3, WIDTH, LOCAL), F32),
            jax.ShapeDtypeStruct((LOCAL, WIDTH), F32),
        ),
        in_specs=[pl.BlockSpec(memory_space=pltpu.SMEM)] + [vmem] * 8,
        out_specs=(vmem,) * 4,
        scratch_shapes=[
            v((ROWS, LOCAL), F32),
            v((ROWS, LOCAL), F32),
            v((HALF, LOCAL), BF16),
            v((2, HALF, LOCAL), BF16),
            v((2, HALF, LOCAL), BF16),
            v((2, 8, LOCAL), F32),
            v((3, WIDTH, WIDTH), BF16),
            v((WIDTH, 3 * WIDTH), BF16),
            v((HALF, WIDTH), BF16),
            v((BALLS, WIDTH, BALL), BF16),
            v((BALLS, WIDTH, BALL), BF16),
            v((BALLS // 2, WIDTH, 2 * BALL), BF16),
            v((HALF, WIDTH), BF16),
            v((2, HALF, LOCAL), F32),
            v((HALF, LOCAL), F32),
            v((BALLS * HEADS, BALL, BALL), F32),
            v((2, LOCAL, 2 * LOCAL), F32),
            v((2, 16, LOCAL), F32),
            v((2, LOCAL, LOCAL), F32),
            v((LEVELS, 256, 256), BF16),
            v((LEVELS, 256, 256), BF16),
            v((256, LOCAL), F32),
            v((256, LOCAL), F32),
            v((2, BALLS, LOCAL), F32),
            v((2, HALF, LOCAL), BF16),
            v((HALF, LOCAL), BF16),
            v((2, HALF, LOCAL), BF16),
            v((1024, WIDTH), F32),
            v((2, 1024, LOCAL), F32),
            v((2, 512, LOCAL), F32),
            v((2, 512, LOCAL), F32),
            v((2, 512, LOCAL), BF16),
            v((16, 2, 32, LOCAL), BF16),
            v((2, 32, LOCAL), F32),
            v((8, 32, LOCAL), F32),
            v((512, LOCAL), F32),
            v((1024, LOCAL), F32),
            v((ROWS, LOCAL), BF16),
            v((ROWS // LOCAL, LOCAL), jnp.int32),
            pltpu.SMEM((ROWS // LOCAL, LOCAL), jnp.int32),
            pltpu.SemaphoreType.DMA,
            sems(1), sems(BALLS), sems(BALLS), sems(BALLS), sems(BALLS), sems(8), sems(16),
            sems(1), sems(1), sems(16), sems(8), sems(16), sems(1),
        ],
        compiler_params=pltpu.CompilerParams(
            collective_id=0, has_side_effects=True, vmem_limit_bytes=58 * 1024 * 1024
        ),
        cost_estimate=pl.CostEstimate(flops=8 * 10**9, bytes_accessed=8 * 10**6, transcendentals=4 * 10**6),
    )(order, order_rows, points, cot, gain, tree_gain, slots, w, wo)


def local(points, order, norm_gain, qkv_weight, out_weight, tree_gain, partner_slot, cotangent):
    return run_main(
        order, order.reshape(ROWS // LOCAL, LOCAL), points, cotangent, norm_gain[None], tree_gain,
        partner_slot.T, qkv_weight, out_weight,
    )


def solution(mesh):
    in_specs = (
        P("pts", "ch"),
        P("pts"),
        P("ch"),
        P(),
        P(),
        P(None, "ch"),
        P("pts", None),
        P("pts", "ch"),
    )
    out_specs = (P("pts", "ch"), P("pts", "ch"), P(None, None, "ch"), P("ch", None))
    return jax.shard_map(local, mesh=mesh, in_specs=in_specs, out_specs=out_specs, check_vma=False)
```

```python
import math

import jax
import jax.numpy as jnp
from jax import lax
from jax.experimental import pallas as pl
from jax.experimental.pallas import tpu as pltpu
from jax.sharding import PartitionSpec as P

HEAD = 32
BALL = 256
LEVELS = 4
EPSILON = 1e-06

ROWS = 4096
HALF = 2048
LOCAL = 128
WIDTH = 256
HEADS = 8
BALLS = 8
GROUP = 16
EARLY_COT = 6

F32 = jnp.float32
BF16 = jnp.bfloat16
MESH = pl.DeviceIdType.MESH
SCALE = HEAD ** (-0.5)
SCALE_LOG2 = SCALE * math.log2(math.e)


def nn(left, right):
    return lax.dot_general(left, right, (((1,), (0,)), ((), ())), preferred_element_type=F32)


def nt(left, right):
    return lax.dot_general(left, right, (((1,), (1,)), ((), ())), preferred_element_type=F32)


def exact_dot(onehot, values):
    high = values.astype(BF16)
    rest = values - high.astype(F32)
    middle = rest.astype(BF16)
    low = (rest - middle.astype(F32)).astype(BF16)
    parts = nn(onehot, jnp.concatenate([high, middle, low], axis=1))
    return parts[:, :LOCAL] + parts[:, LOCAL:2 * LOCAL] + parts[:, 2 * LOCAL:]


def main_kernel(
    order_ref, order_rows, points, cot, gain_ref, tree_gain_ref, slots_t, w, wo,
    mixed, point_grad, qkv_out, out_out,
    wide, moved, theirs_rows, xh, cth, sm, wt, wcat, vn, q_t, k_t, att_t, nrm, hid, inv, probs,
    early, chip_nodes, nodes, picks, picks_t, final_state, final_grad, node_grads,
    pstage, precv, gstage, acc_t,
    acc, recv_a, sum_a, half_a, recv_c, sum_c, recv_z, all_f, total,
    grads, places, places_smem, s_places,
    s_small, s_pts, s_cot, s_proj, s_grad, s_early, s_tree, s_ng, s_a, s_c, s_z, s_f, s_g,
):
    p = lax.axis_index("pts")
    c = lax.axis_index("ch")
    core = p % 2
    plane = (p // 2) % 16
    depth = p // 32
    other_c = 1 - c
    local_range = p % GROUP
    chip = local_range // 2
    group_base = (p // GROUP) * GROUP
    ring = depth * 2 + c
    pair = (p, other_c)
    sibling = (p + 1 - 2 * core, c)

    def tree_peer(distance):
        there = (chip * 2 + c + distance) % 16
        return (group_base + (there // 2) * 2 + core, there % 2)

    def early_peer(distance):
        return (group_base + ((chip + distance) % 8) * 2 + core, c)

    def plane_index(distance):
        return (plane + distance) % 16

    def plane_peer(distance):
        return (depth * 32 + plane_index(distance) * 2 + core, c)

    def ring_peer(distance):
        there = (ring + distance) % 8
        return ((there // 2) * 32 + plane * 2 + core, there % 2)

    barrier = pltpu.get_barrier_semaphore()

    def greet(target):
        pl.semaphore_signal(barrier, inc=1, device_id=target, device_id_type=MESH)

    greet(sibling)
    for distance in range(1, 16):
        greet(tree_peer(distance))
    far_base = (1 - plane // 8) * 8
    for step in range(8):
        greet((depth * 32 + (far_base + step) * 2 + core, c))
    for step in range(1, 4):
        for half in range(2):
            greet((((depth + step) % 4) * 32 + plane * 2 + core, half))

    def send(src, dst, sems, index, target):
        return pltpu.make_async_remote_copy(
            src_ref=src, dst_ref=dst, send_sem=sems.at[0, index], recv_sem=sems.at[1, index],
            device_id=target, device_id_type=MESH,
        )

    def theirs(ball):
        return pl.ds(pl.multiple_of(other_c * HALF + ball * BALL, BALL), BALL)

    def ours(ball):
        return pl.ds(pl.multiple_of(c * HALF + ball * BALL, BALL), BALL)

    def here(ball):
        return pl.ds(pl.multiple_of(ball * BALL, BALL), BALL)

    def small_copy():
        return send(sm.at[c], sm.at[c], s_small, 0, pair)

    def points_copy(ball):
        return send(theirs_rows.at[here(ball)], xh.at[c, here(ball)], s_pts, ball, pair)

    def cot_copy(ball):
        return send(cot.at[theirs(ball)], cth.at[c, here(ball)], s_cot, ball, pair)

    def proj_copy(ball):
        return send(pstage.at[other_c, here(ball)], precv.at[here(ball)], s_proj, ball, pair)

    def grad_copy(ball):
        return send(gstage.at[other_c, here(ball)], grads.at[ours(ball)], s_grad, ball, pair)

    def both(ref, rows):
        return jnp.concatenate([ref[0, rows, :], ref[1, rows, :]], axis=1).astype(F32)

    wide[...] = points[...].astype(F32)

    def pick_rows(start):
        def step(block, carry):
            base = start + block * 16
            for inner in range(16):
                row = order_ref[base + inner]
                moved[pl.ds(base + inner, 1), :] = wide[pl.ds(row, 1), :]
            return carry

        lax.fori_loop(0, BALL // 16, step, 0)
        return moved[pl.ds(pl.multiple_of(start, BALL), BALL), :].astype(BF16)

    def their_ball(ball, carry):
        theirs_rows[here(ball), :] = pick_rows(other_c * HALF + ball * BALL)
        points_copy(ball).start()
        return carry

    theirs_rows[0:BALL, :] = pick_rows(other_c * HALF)
    own_small = jnp.concatenate([gain_ref[...], tree_gain_ref[...], jnp.zeros((3, LOCAL), F32)], axis=0)
    sm[pl.ds(c, 1)] = own_small[None]
    pl.semaphore_wait(barrier, 30)
    small_copy().start()
    points_copy(0).start()
    lax.fori_loop(1, BALLS, their_ball, 0)

    slots = jnp.transpose(
        jnp.concatenate(
            [
                jnp.concatenate([slots_t[...].astype(F32), jnp.zeros((LEVELS, LOCAL - 16), F32)], axis=1),
                jnp.zeros((LOCAL - LEVELS, LOCAL), F32),
            ],
            axis=0,
        )
    )
    range_rows = pl.ds(pl.multiple_of(local_range * BALLS, BALLS), BALLS)
    chip_rows = pl.ds(pl.multiple_of(chip * 16, 16), 16)
    for half in range(2):
        sums = [
            jnp.sum(cot[ball * BALL:(ball + 1) * BALL, :].astype(F32), axis=0, keepdims=True)
            for ball in range(half * BALLS, (half + 1) * BALLS)
        ]
        early[half, range_rows, 0:LOCAL] = jnp.concatenate(sums, axis=0)
        early[half, range_rows, LOCAL:] = slots[half * BALLS:(half + 1) * BALLS, :]

    def early_first():
        block = early.at[:, range_rows]
        return send(block, block, s_early, 0, sibling)

    def early_copy(distance):
        block = early.at[:, chip_rows]
        return send(block, block, s_early, distance, early_peer(distance))

    early_first().start()

    cth[pl.ds(c, 1)] = cot[pl.ds(pl.multiple_of(c * HALF, HALF), HALF), :][None]
    for index in range(3):
        wt[index] = jnp.transpose(w[index])
        wcat[:, index * WIDTH:(index + 1) * WIDTH] = w[index]

    def own_ball(ball, carry):
        xh[pl.ds(c, 1), here(ball), :] = pick_rows(c * HALF + ball * BALL)[None]
        return carry

    lax.fori_loop(0, BALLS, own_ball, 0)
    early_first().wait_recv()
    for distance in range(1, 8):
        early_copy(distance).start()
    small_copy().wait_recv()
    gain = jnp.concatenate([sm[0, 0:1, :], sm[1, 0:1, :]], axis=1)
    bands = [slice(head * HEAD, (head + 1) * HEAD) for head in range(HEADS)]

    def two(step):
        return pl.ds(pl.multiple_of(step * 2 * BALL, 2 * BALL), 2 * BALL)

    pieces = [(side, band) for side in range(2) for band in bands]
    sides = [slice(0, BALL), slice(BALL, 2 * BALL)]

    def forward(step, carry):
        rows = two(step)
        for side in range(2):
            points_copy(2 * step + side).wait_recv()

        @pl.when(step < EARLY_COT // 2)
        def _():
            for side in range(2):
                cot_copy(2 * step + side).start()

        ordered = both(xh, rows)
        mean = jnp.sum(ordered * ordered, axis=1, keepdims=True) * (1.0 / WIDTH)
        inverse = lax.rsqrt(mean + EPSILON)
        normed = (ordered * inverse * gain).astype(BF16)
        keyset = nn(normed, w[1]).astype(BF16)
        query_t = nt(wt[0], normed).astype(BF16)
        value_t = nt(wt[2], normed).astype(BF16)
        scores = [nn(keyset[sides[side], band], query_t[band, sides[side]]) for side, band in pieces]
        key_t = nt(wt[1], normed).astype(BF16)
        value = nn(normed, w[2]).astype(BF16)
        halves = []
        for index in range(2 * HEADS):
            top = jnp.max(scores[index], axis=0, keepdims=True)
            weights = jnp.exp2((scores[index] - top) * SCALE_LOG2)
            scaled = weights * (1.0 / jnp.sum(weights, axis=0, keepdims=True))
            probs[step * 2 * HEADS + index] = scaled
            halves.append(scaled.astype(BF16))
        parts = [
            nn(value_t[band, sides[side]], half).astype(BF16) for (side, band), half in zip(pieces, halves)
        ]
        attended_t = jnp.concatenate(
            [jnp.concatenate(parts[:HEADS], axis=0), jnp.concatenate(parts[HEADS:], axis=0)], axis=1
        )
        projected = nn(jnp.transpose(attended_t), wo[...])
        hidden = ordered + projected
        for side in range(2):
            node = jnp.sum(hidden[sides[side], :], axis=0, keepdims=True) * BALL ** (-0.5)
            row = pl.ds(core * BALLS + 2 * step + side, 1)
            chip_nodes[0, row, :] = node[:, :LOCAL]
            chip_nodes[1, row, :] = node[:, LOCAL:]
            q_t[2 * step + side] = query_t[:, sides[side]]
            k_t[2 * step + side] = key_t[:, sides[side]]
        hid[0, rows, :] = hidden[:, :LOCAL]
        hid[1, rows, :] = hidden[:, LOCAL:]
        pstage[0, rows, :] = projected[:, :LOCAL].astype(BF16)
        pstage[1, rows, :] = projected[:, LOCAL:].astype(BF16)
        inv[rows, :] = jnp.broadcast_to(inverse, (2 * BALL, LOCAL))
        nrm[rows, :] = normed
        vn[rows, :] = value
        att_t[step] = attended_t
        return carry

    lax.fori_loop(0, BALLS // 2, forward, 0)

    core_rows = pl.ds(pl.multiple_of(core * BALLS, BALLS), BALLS)

    def tree_first():
        block = chip_nodes.at[:, core_rows]
        return send(block, block, s_tree, 0, sibling)

    def tree_copy(distance):
        return send(
            chip_nodes.at[(c + distance) % 2], nodes.at[c, chip_rows], s_tree, distance, tree_peer(distance)
        )

    tree_first().start()
    tree_first().wait_recv()
    for distance in range(1, 16):
        tree_copy(distance).start()
    for ball in range(EARLY_COT, BALLS):
        cot_copy(ball).start()
    nodes[pl.ds(c, 1), chip_rows, :] = chip_nodes[pl.ds(c, 1)]

    for distance in range(1, 8):
        early_copy(distance).wait_recv()
    count = GROUP * 16
    range_ids = (lax.broadcasted_iota(jnp.int32, (count, 1), 0) % LOCAL) // BALLS
    lane_ids = lax.broadcasted_iota(jnp.int32, (count, count), 1)
    known = jnp.concatenate([early[0], early[1]], axis=0)
    for level in range(LEVELS):
        slot = known[:, LOCAL + level:LOCAL + level + 1].astype(jnp.int32)
        bit = (range_ids // (1 << level)) % 2
        partner = (slot // BALLS) * LOCAL + (range_ids + (1 - 2 * bit) * (1 << level)) * BALLS + slot % BALLS
        onehot = jnp.where(lane_ids == partner, 1.0, 0.0).astype(BF16)
        picks[level] = onehot
        picks_t[level] = jnp.transpose(onehot)
    acc_t[...] = jnp.zeros_like(acc_t)
    own_gains = sm[pl.ds(c, 1)][0]

    for distance in range(1, 16):
        tree_copy(distance).wait_recv()
    states = jnp.concatenate([nodes[0], nodes[1]], axis=0)
    chosen_list = []
    for level in range(LEVELS):
        chosen = exact_dot(picks[level], states)
        states = states + own_gains[1 + level:2 + level, :] * (chosen * jax.nn.sigmoid(chosen))
        chosen_list.append(chosen)
    node_grad = known[:, 0:LOCAL]
    for level in reversed(range(LEVELS)):
        chosen = chosen_list[level]
        sigma = jax.nn.sigmoid(chosen)
        slope = sigma * (1.0 + chosen * (1.0 - sigma))
        node_grad = node_grad + exact_dot(
            picks_t[level], own_gains[1 + level:2 + level, :] * slope * node_grad
        )
    final_grad[...] = node_grad
    final_state[...] = states

    def range_row(half, ball):
        return half * LOCAL + local_range * BALLS + ball

    def ng_copy():
        part = final_grad.at[pl.ds(pl.multiple_of(range_row(other_c, 0), BALLS), BALLS)]
        return send(part, node_grads.at[c], s_ng, 0, pair)

    ng_copy().start()
    for ball in range(BALLS):
        proj_copy(ball).start()
    node_grads[pl.ds(c, 1)] = final_grad[pl.ds(pl.multiple_of(range_row(c, 0), BALLS), BALLS), :][None]

    def own_mixed(ball, carry):
        state = final_state[pl.ds(range_row(c, ball), 1), :]
        mixed[ours(ball), :] = (hid[pl.ds(c, 1), here(ball), :][0] + state).astype(BF16)
        return carry

    lax.fori_loop(0, BALLS, own_mixed, 0)
    ng_copy().wait_recv()

    def backward(step, carry):
        rows = two(step)
        shifts = []
        for side in range(2):
            cot_copy(2 * step + side).wait_recv()
            row = pl.ds(2 * step + side, 1)
            shift = jnp.concatenate([node_grads[0, row, :], node_grads[1, row, :]], axis=1) * BALL ** (-0.5)
            shifts.append(jnp.broadcast_to(shift, (BALL, WIDTH)))
        hidden_grad = (both(cth, rows) + jnp.concatenate(shifts, axis=0)).astype(BF16)
        att_grad = nt(wo[...], hidden_grad).astype(BF16)
        value = vn[rows, :]
        prob_grads = [nn(value[sides[side], band], att_grad[band, sides[side]]) for side, band in pieces]
        acc_t[768:1024, :] += nn(att_t[step], hidden_grad)
        score_grads, halves = [], []
        for index in range(2 * HEADS):
            prob = probs[step * 2 * HEADS + index]
            dots = jnp.sum(prob_grads[index] * prob, axis=0, keepdims=True)
            score_grads.append((prob * (prob_grads[index] - dots) * SCALE).astype(BF16))
            halves.append(prob.astype(BF16))
        dv = [
            nt(att_grad[band, sides[side]], half).astype(BF16) for (side, band), half in zip(pieces, halves)
        ]
        dq = [
            nn(k_t[2 * step + side, band, :], part).astype(BF16)
            for (side, band), part in zip(pieces, score_grads)
        ]
        dk = [
            nt(q_t[2 * step + side, band, :], part).astype(BF16)
            for (side, band), part in zip(pieces, score_grads)
        ]
        all_grads = jnp.concatenate(
            [
                jnp.concatenate(dq[:HEADS] + dk[:HEADS] + dv[:HEADS], axis=0),
                jnp.concatenate(dq[HEADS:] + dk[HEADS:] + dv[HEADS:], axis=0),
            ],
            axis=1,
        )
        normed_grad = nn(wcat[...], all_grads)
        acc_t[0:768, :] += nn(all_grads, nrm[rows, :])
        scaled_grad = jnp.transpose(normed_grad) * gain
        ordered = both(xh, rows)
        inverse = jnp.concatenate([inv[rows, :], inv[rows, :]], axis=1)
        correction = jnp.sum(ordered * scaled_grad, axis=1, keepdims=True) * (1.0 / WIDTH)
        ordered_grad = (
            hidden_grad.astype(F32) + inverse * scaled_grad - ordered * (inverse * inverse * inverse) * correction
        ).astype(BF16)
        gstage[0, rows, :] = ordered_grad[:, :LOCAL]
        gstage[1, rows, :] = ordered_grad[:, LOCAL:]
        for side in range(2):
            grad_copy(2 * step + side).start()
        own = pl.ds(pl.multiple_of(c * HALF + step * 2 * BALL, 2 * BALL), 2 * BALL)
        grads[own, :] = gstage[pl.ds(c, 1), rows, :][0]
        return carry

    lax.fori_loop(0, BALLS // 2, backward, 0)

    for index in range(3):
        part = jnp.transpose(acc_t[index * 256:(index + 1) * 256, :])
        acc[0, index * 256:(index + 1) * 256, :] = part[:, :LOCAL]
        acc[1, index * 256:(index + 1) * 256, :] = part[:, LOCAL:]
    for half in range(2):
        band = slice(768 + half * LOCAL, 768 + (half + 1) * LOCAL)
        acc[half, 768:896, :] = acc_t[band, :LOCAL]
        acc[half, 896:1024, :] = acc_t[band, LOCAL:]

    kept = pl.ds(pl.multiple_of(core * 512, 512), 512)
    given = pl.ds(pl.multiple_of((1 - core) * 512, 512), 512)
    copy_a = send(acc.at[:, given], recv_a, s_a, 0, sibling)
    copy_a.start()

    tiles = ROWS // LOCAL
    lanes = lax.broadcasted_iota(jnp.int32, (1, LOCAL), 1)
    high_ids = lax.broadcasted_iota(jnp.int32, (tiles, LOCAL), 0)
    low_ids = lax.broadcasted_iota(jnp.int32, (LOCAL, LOCAL), 0)
    high_hits, low_hits = [], []
    for tile in range(tiles):
        target = order_rows[tile:tile + 1, :]
        high_hits.append(jnp.where(high_ids == target // LOCAL, 1.0, 0.0).astype(BF16))
        hit = low_ids == target % LOCAL
        source = lanes + tile * LOCAL
        low_hits.append(
            jnp.concatenate(
                [
                    jnp.where(hit, (source // 64).astype(F32), 0.0),
                    jnp.where(hit, (source % 64).astype(F32), 0.0),
                ],
                axis=0,
            ).astype(BF16)
        )
    found = nt(jnp.concatenate(high_hits, axis=1), jnp.concatenate(low_hits, axis=1))
    inverse_order = (found[:, :LOCAL] * 64.0 + found[:, LOCAL:]).astype(jnp.int32)
    places[...] = jnp.clip(inverse_order, 0, ROWS - 1)
    fetch = pltpu.make_async_copy(places, places_smem, s_places)
    fetch.start()

    def return_rows(start, stop):
        def step(block, carry):
            for inner in range(16):
                row = places_smem[block // 8, (block % 8) * 16 + inner]
                moved[pl.ds(block * 16 + inner, 1), :] = wide[pl.ds(row, 1), :]
            return carry

        lax.fori_loop(start // 16, stop // 16, step, 0)
        point_grad[start:stop, :] = moved[start:stop, :].astype(BF16)

    def their_mixed(ball, carry):
        rows = here(ball)
        proj_copy(ball).wait_recv()
        state = final_state[pl.ds(range_row(other_c, ball), 1), :]
        mixed[theirs(ball), :] = (
            theirs_rows[rows, :].astype(F32) + precv[rows, :].astype(F32) + state
        ).astype(BF16)
        return carry

    small_copy().wait_send()
    ng_copy().wait_send()

    def settle_early(ball, carry):
        points_copy(ball).wait_send()
        cot_copy(ball).wait_send()
        return carry

    lax.fori_loop(0, BALLS, settle_early, 0)
    tree_first().wait_send()
    early_first().wait_send()
    for distance in range(1, 8):
        early_copy(distance).wait_send()
    for distance in range(1, 16):
        tree_copy(distance).wait_send()

    copy_a.wait_recv()
    sum_a[...] = acc[:, kept, :] + recv_a[...]
    half_a[...] = sum_a[...].astype(BF16)

    def copy_c(distance):
        piece = pl.ds(pl.multiple_of(plane_index(distance) * 32, 32), 32)
        return send(half_a.at[:, piece], recv_c.at[distance], s_c, distance, plane_peer(distance))

    for distance in range(1, 16):
        copy_c(distance).start()
    lax.fori_loop(0, BALLS, their_mixed, 0)
    for ball in range(BALLS):
        grad_copy(ball).wait_recv()
    wide[...] = grads[...].astype(F32)
    part = sum_a[:, pl.ds(pl.multiple_of(plane * 32, 32), 32), :]
    for distance in range(1, 16):
        copy_c(distance).wait_recv()
        part = part + recv_c[distance].astype(F32)
    sum_c[...] = part

    def copy_z(distance):
        return send(sum_c.at[(ring + distance) % 2], recv_z.at[ring], s_z, distance, ring_peer(distance))

    for distance in range(1, 8):
        copy_z(distance).start()
    recv_z[pl.ds(ring, 1)] = sum_c[pl.ds(c, 1)]
    for distance in range(1, 16):
        copy_c(distance).wait_send()
    fetch.wait()
    return_rows(0, HALF)
    for distance in range(1, 8):
        copy_z(distance).wait_recv()
    part = recv_z[0]
    for step in range(1, 8):
        part = part + recv_z[step]
    plane_rows = pl.ds(pl.multiple_of(plane * 32, 32), 32)
    all_f[plane_rows, :] = part

    def copy_f(distance):
        return send(all_f.at[plane_rows], all_f.at[plane_rows], s_f, distance, plane_peer(distance))

    for distance in range(1, 16):
        copy_f(distance).start()
    return_rows(HALF, ROWS)
    for distance in range(1, 16):
        copy_f(distance).wait_recv()

    copy_g = send(all_f, total.at[kept], s_g, 0, sibling)
    copy_g.start()
    total[kept, :] = all_f[...]
    copy_g.wait_recv()
    for index in range(3):
        qkv_out[index] = total[index * 256:(index + 1) * 256, :]
    out_out[:, :LOCAL] = total[768:896, :]
    out_out[:, LOCAL:] = total[896:1024, :]

    def settle(ball, carry):
        proj_copy(ball).wait_send()
        grad_copy(ball).wait_send()
        return carry

    lax.fori_loop(0, BALLS, settle, 0)
    copy_a.wait_send()
    for distance in range(1, 16):
        copy_f(distance).wait_send()
    for distance in range(1, 8):
        copy_z(distance).wait_send()
    copy_g.wait_send()


def run_main(order, order_rows, points, cot, gain, tree_gain, slots, w, wo):
    vmem = pl.BlockSpec(memory_space=pltpu.VMEM)
    sems = lambda count: pltpu.SemaphoreType.DMA((2, count))
    v = pltpu.VMEM
    return pl.pallas_call(
        main_kernel,
        out_shape=(
            jax.ShapeDtypeStruct((ROWS, LOCAL), BF16),
            jax.ShapeDtypeStruct((ROWS, LOCAL), BF16),
            jax.ShapeDtypeStruct((3, WIDTH, LOCAL), F32),
            jax.ShapeDtypeStruct((LOCAL, WIDTH), F32),
        ),
        in_specs=[pl.BlockSpec(memory_space=pltpu.SMEM)] + [vmem] * 8,
        out_specs=(vmem,) * 4,
        scratch_shapes=[
            v((ROWS, LOCAL), F32),
            v((ROWS, LOCAL), F32),
            v((HALF, LOCAL), BF16),
            v((2, HALF, LOCAL), BF16),
            v((2, HALF, LOCAL), BF16),
            v((2, 8, LOCAL), F32),
            v((3, WIDTH, WIDTH), BF16),
            v((WIDTH, 3 * WIDTH), BF16),
            v((HALF, WIDTH), BF16),
            v((BALLS, WIDTH, BALL), BF16),
            v((BALLS, WIDTH, BALL), BF16),
            v((BALLS // 2, WIDTH, 2 * BALL), BF16),
            v((HALF, WIDTH), BF16),
            v((2, HALF, LOCAL), F32),
            v((HALF, LOCAL), F32),
            v((BALLS * HEADS, BALL, BALL), F32),
            v((2, LOCAL, 2 * LOCAL), F32),
            v((2, 16, LOCAL), F32),
            v((2, LOCAL, LOCAL), F32),
            v((LEVELS, 256, 256), BF16),
            v((LEVELS, 256, 256), BF16),
            v((256, LOCAL), F32),
            v((256, LOCAL), F32),
            v((2, BALLS, LOCAL), F32),
            v((2, HALF, LOCAL), BF16),
            v((HALF, LOCAL), BF16),
            v((2, HALF, LOCAL), BF16),
            v((1024, WIDTH), F32),
            v((2, 1024, LOCAL), F32),
            v((2, 512, LOCAL), F32),
            v((2, 512, LOCAL), F32),
            v((2, 512, LOCAL), BF16),
            v((16, 2, 32, LOCAL), BF16),
            v((2, 32, LOCAL), F32),
            v((8, 32, LOCAL), F32),
            v((512, LOCAL), F32),
            v((1024, LOCAL), F32),
            v((ROWS, LOCAL), BF16),
            v((ROWS // LOCAL, LOCAL), jnp.int32),
            pltpu.SMEM((ROWS // LOCAL, LOCAL), jnp.int32),
            pltpu.SemaphoreType.DMA,
            sems(1), sems(BALLS), sems(BALLS), sems(BALLS), sems(BALLS), sems(8), sems(16),
            sems(1), sems(1), sems(16), sems(8), sems(16), sems(1),
        ],
        compiler_params=pltpu.CompilerParams(
            collective_id=0, has_side_effects=True, vmem_limit_bytes=58 * 1024 * 1024
        ),
        cost_estimate=pl.CostEstimate(flops=8 * 10**9, bytes_accessed=8 * 10**6, transcendentals=4 * 10**6),
    )(order, order_rows, points, cot, gain, tree_gain, slots, w, wo)


def local(points, order, norm_gain, qkv_weight, out_weight, tree_gain, partner_slot, cotangent):
    return run_main(
        order, order.reshape(ROWS // LOCAL, LOCAL), points, cotangent, norm_gain[None], tree_gain,
        partner_slot.T, qkv_weight, out_weight,
    )


def solution(mesh):
    in_specs = (
        P("pts", "ch"),
        P("pts"),
        P("ch"),
        P(),
        P(),
        P(None, "ch"),
        P("pts", None),
        P("pts", "ch"),
    )
    out_specs = (P("pts", "ch"), P("pts", "ch"), P(None, None, "ch"), P("ch", None))
    return jax.shard_map(local, mesh=mesh, in_specs=in_specs, out_specs=out_specs, check_vma=False)
```

```python
import math

import jax
import jax.numpy as jnp
from jax import lax
from jax.experimental import pallas as pl
from jax.experimental.pallas import tpu as pltpu
from jax.sharding import PartitionSpec as P

HEAD = 32
BALL = 256
LEVELS = 4
EPSILON = 1e-06

ROWS = 4096
HALF = 2048
LOCAL = 128
WIDTH = 256
HEADS = 8
BALLS = 8
GROUP = 16
EARLY_COT = 4

F32 = jnp.float32
BF16 = jnp.bfloat16
MESH = pl.DeviceIdType.MESH
SCALE = HEAD ** (-0.5)
SCALE_LOG2 = SCALE * math.log2(math.e)


def nn(left, right):
    return lax.dot_general(left, right, (((1,), (0,)), ((), ())), preferred_element_type=F32)


def nt(left, right):
    return lax.dot_general(left, right, (((1,), (1,)), ((), ())), preferred_element_type=F32)


def exact_dot(onehot, values):
    high = values.astype(BF16)
    rest = values - high.astype(F32)
    middle = rest.astype(BF16)
    low = (rest - middle.astype(F32)).astype(BF16)
    parts = nn(onehot, jnp.concatenate([high, middle, low], axis=1))
    return parts[:, :LOCAL] + parts[:, LOCAL:2 * LOCAL] + parts[:, 2 * LOCAL:]


def main_kernel(
    order_ref, order_rows, points, cot, gain_ref, tree_gain_ref, slots_t, w, wo,
    mixed, point_grad, qkv_out, out_out,
    wide, moved, theirs_rows, xh, cth, sm, wt, wcat, vn, q_t, k_t, att_t, nrm, hid, inv, probs,
    early, chip_nodes, nodes, picks, picks_t, final_state, final_grad, node_grads,
    pstage, precv, gstage, acc_t,
    acc, recv_a, sum_a, half_a, recv_c, sum_c, recv_z, all_f, total,
    grads, places, places_smem, s_places,
    s_small, s_pts, s_cot, s_proj, s_grad, s_early, s_tree, s_ng, s_a, s_c, s_z, s_f, s_g,
):
    p = lax.axis_index("pts")
    c = lax.axis_index("ch")
    core = p % 2
    plane = (p // 2) % 16
    depth = p // 32
    other_c = 1 - c
    local_range = p % GROUP
    chip = local_range // 2
    group_base = (p // GROUP) * GROUP
    ring = depth * 2 + c
    pair = (p, other_c)
    sibling = (p + 1 - 2 * core, c)

    def tree_peer(distance):
        there = (chip * 2 + c + distance) % 16
        return (group_base + (there // 2) * 2 + core, there % 2)

    def early_peer(distance):
        return (group_base + ((chip + distance) % 8) * 2 + core, c)

    def plane_index(distance):
        return (plane + distance) % 16

    def plane_peer(distance):
        return (depth * 32 + plane_index(distance) * 2 + core, c)

    def ring_peer(distance):
        there = (ring + distance) % 8
        return ((there // 2) * 32 + plane * 2 + core, there % 2)

    barrier = pltpu.get_barrier_semaphore()

    def greet(target):
        pl.semaphore_signal(barrier, inc=1, device_id=target, device_id_type=MESH)

    greet(sibling)
    for distance in range(1, 16):
        greet(tree_peer(distance))
    far_base = (1 - plane // 8) * 8
    for step in range(8):
        greet((depth * 32 + (far_base + step) * 2 + core, c))
    for step in range(1, 4):
        for half in range(2):
            greet((((depth + step) % 4) * 32 + plane * 2 + core, half))

    def send(src, dst, sems, index, target):
        return pltpu.make_async_remote_copy(
            src_ref=src, dst_ref=dst, send_sem=sems.at[0, index], recv_sem=sems.at[1, index],
            device_id=target, device_id_type=MESH,
        )

    def theirs(ball):
        return pl.ds(pl.multiple_of(other_c * HALF + ball * BALL, BALL), BALL)

    def ours(ball):
        return pl.ds(pl.multiple_of(c * HALF + ball * BALL, BALL), BALL)

    def here(ball):
        return pl.ds(pl.multiple_of(ball * BALL, BALL), BALL)

    def small_copy():
        return send(sm.at[c], sm.at[c], s_small, 0, pair)

    def points_copy(ball):
        return send(theirs_rows.at[here(ball)], xh.at[c, here(ball)], s_pts, ball, pair)

    def cot_copy(ball):
        return send(cot.at[theirs(ball)], cth.at[c, here(ball)], s_cot, ball, pair)

    def proj_copy(ball):
        return send(pstage.at[other_c, here(ball)], precv.at[here(ball)], s_proj, ball, pair)

    def grad_copy(ball):
        return send(gstage.at[other_c, here(ball)], grads.at[ours(ball)], s_grad, ball, pair)

    def both(ref, rows):
        return jnp.concatenate([ref[0, rows, :], ref[1, rows, :]], axis=1).astype(F32)

    wide[...] = points[...].astype(F32)

    def pick_rows(start):
        def step(block, carry):
            base = start + block * 16
            for inner in range(16):
                row = order_ref[base + inner]
                moved[pl.ds(base + inner, 1), :] = wide[pl.ds(row, 1), :]
            return carry

        lax.fori_loop(0, BALL // 16, step, 0)
        return moved[pl.ds(pl.multiple_of(start, BALL), BALL), :].astype(BF16)

    def their_ball(ball, carry):
        theirs_rows[here(ball), :] = pick_rows(other_c * HALF + ball * BALL)
        points_copy(ball).start()
        return carry

    theirs_rows[0:BALL, :] = pick_rows(other_c * HALF)
    own_small = jnp.concatenate([gain_ref[...], tree_gain_ref[...], jnp.zeros((3, LOCAL), F32)], axis=0)
    sm[pl.ds(c, 1)] = own_small[None]
    pl.semaphore_wait(barrier, 30)
    small_copy().start()
    points_copy(0).start()
    lax.fori_loop(1, BALLS, their_ball, 0)

    slots = jnp.transpose(
        jnp.concatenate(
            [
                jnp.concatenate([slots_t[...].astype(F32), jnp.zeros((LEVELS, LOCAL - 16), F32)], axis=1),
                jnp.zeros((LOCAL - LEVELS, LOCAL), F32),
            ],
            axis=0,
        )
    )
    range_rows = pl.ds(pl.multiple_of(local_range * BALLS, BALLS), BALLS)
    chip_rows = pl.ds(pl.multiple_of(chip * 16, 16), 16)
    for half in range(2):
        sums = [
            jnp.sum(cot[ball * BALL:(ball + 1) * BALL, :].astype(F32), axis=0, keepdims=True)
            for ball in range(half * BALLS, (half + 1) * BALLS)
        ]
        early[half, range_rows, 0:LOCAL] = jnp.concatenate(sums, axis=0)
        early[half, range_rows, LOCAL:] = slots[half * BALLS:(half + 1) * BALLS, :]

    def early_first():
        block = early.at[:, range_rows]
        return send(block, block, s_early, 0, sibling)

    def early_copy(distance):
        block = early.at[:, chip_rows]
        return send(block, block, s_early, distance, early_peer(distance))

    early_first().start()

    cth[pl.ds(c, 1)] = cot[pl.ds(pl.multiple_of(c * HALF, HALF), HALF), :][None]
    for index in range(3):
        wt[index] = jnp.transpose(w[index])
        wcat[:, index * WIDTH:(index + 1) * WIDTH] = w[index]

    def own_ball(ball, carry):
        xh[pl.ds(c, 1), here(ball), :] = pick_rows(c * HALF + ball * BALL)[None]
        return carry

    lax.fori_loop(0, BALLS, own_ball, 0)
    early_first().wait_recv()
    for distance in range(1, 8):
        early_copy(distance).start()
    small_copy().wait_recv()
    gain = jnp.concatenate([sm[0, 0:1, :], sm[1, 0:1, :]], axis=1)
    bands = [slice(head * HEAD, (head + 1) * HEAD) for head in range(HEADS)]

    def two(step):
        return pl.ds(pl.multiple_of(step * 2 * BALL, 2 * BALL), 2 * BALL)

    pieces = [(side, band) for side in range(2) for band in bands]
    sides = [slice(0, BALL), slice(BALL, 2 * BALL)]

    def forward(step, carry):
        rows = two(step)
        for side in range(2):
            points_copy(2 * step + side).wait_recv()

        @pl.when(step < EARLY_COT // 2)
        def _():
            for side in range(2):
                cot_copy(2 * step + side).start()

        ordered = both(xh, rows)
        mean = jnp.sum(ordered * ordered, axis=1, keepdims=True) * (1.0 / WIDTH)
        inverse = lax.rsqrt(mean + EPSILON)
        normed = (ordered * inverse * gain).astype(BF16)
        keyset = nn(normed, w[1]).astype(BF16)
        query_t = nt(wt[0], normed).astype(BF16)
        value_t = nt(wt[2], normed).astype(BF16)
        scores = [nn(keyset[sides[side], band], query_t[band, sides[side]]) for side, band in pieces]
        key_t = nt(wt[1], normed).astype(BF16)
        value = nn(normed, w[2]).astype(BF16)
        halves = []
        for index in range(2 * HEADS):
            top = jnp.max(scores[index], axis=0, keepdims=True)
            weights = jnp.exp2((scores[index] - top) * SCALE_LOG2)
            scaled = weights * (1.0 / jnp.sum(weights, axis=0, keepdims=True))
            probs[step * 2 * HEADS + index] = scaled
            halves.append(scaled.astype(BF16))
        parts = [
            nn(value_t[band, sides[side]], half).astype(BF16) for (side, band), half in zip(pieces, halves)
        ]
        attended_t = jnp.concatenate(
            [jnp.concatenate(parts[:HEADS], axis=0), jnp.concatenate(parts[HEADS:], axis=0)], axis=1
        )
        projected = nn(jnp.transpose(attended_t), wo[...])
        hidden = ordered + projected
        for side in range(2):
            node = jnp.sum(hidden[sides[side], :], axis=0, keepdims=True) * BALL ** (-0.5)
            row = pl.ds(core * BALLS + 2 * step + side, 1)
            chip_nodes[0, row, :] = node[:, :LOCAL]
            chip_nodes[1, row, :] = node[:, LOCAL:]
            q_t[2 * step + side] = query_t[:, sides[side]]
            k_t[2 * step + side] = key_t[:, sides[side]]
        hid[0, rows, :] = hidden[:, :LOCAL]
        hid[1, rows, :] = hidden[:, LOCAL:]
        pstage[0, rows, :] = projected[:, :LOCAL].astype(BF16)
        pstage[1, rows, :] = projected[:, LOCAL:].astype(BF16)
        inv[rows, :] = jnp.broadcast_to(inverse, (2 * BALL, LOCAL))
        nrm[rows, :] = normed
        vn[rows, :] = value
        att_t[step] = attended_t
        return carry

    lax.fori_loop(0, BALLS // 2, forward, 0)

    core_rows = pl.ds(pl.multiple_of(core * BALLS, BALLS), BALLS)

    def tree_first():
        block = chip_nodes.at[:, core_rows]
        return send(block, block, s_tree, 0, sibling)

    def tree_copy(distance):
        return send(
            chip_nodes.at[(c + distance) % 2], nodes.at[c, chip_rows], s_tree, distance, tree_peer(distance)
        )

    tree_first().start()
    tree_first().wait_recv()
    for distance in range(1, 16):
        tree_copy(distance).start()
    for ball in range(EARLY_COT, BALLS):
        cot_copy(ball).start()
    nodes[pl.ds(c, 1), chip_rows, :] = chip_nodes[pl.ds(c, 1)]

    for distance in range(1, 8):
        early_copy(distance).wait_recv()
    count = GROUP * 16
    range_ids = (lax.broadcasted_iota(jnp.int32, (count, 1), 0) % LOCAL) // BALLS
    lane_ids = lax.broadcasted_iota(jnp.int32, (count, count), 1)
    known = jnp.concatenate([early[0], early[1]], axis=0)
    for level in range(LEVELS):
        slot = known[:, LOCAL + level:LOCAL + level + 1].astype(jnp.int32)
        bit = (range_ids // (1 << level)) % 2
        partner = (slot // BALLS) * LOCAL + (range_ids + (1 - 2 * bit) * (1 << level)) * BALLS + slot % BALLS
        onehot = jnp.where(lane_ids == partner, 1.0, 0.0).astype(BF16)
        picks[level] = onehot
        picks_t[level] = jnp.transpose(onehot)
    acc_t[...] = jnp.zeros_like(acc_t)
    own_gains = sm[pl.ds(c, 1)][0]

    for distance in range(1, 16):
        tree_copy(distance).wait_recv()
    states = jnp.concatenate([nodes[0], nodes[1]], axis=0)
    chosen_list = []
    for level in range(LEVELS):
        chosen = exact_dot(picks[level], states)
        states = states + own_gains[1 + level:2 + level, :] * (chosen * jax.nn.sigmoid(chosen))
        chosen_list.append(chosen)
    node_grad = known[:, 0:LOCAL]
    for level in reversed(range(LEVELS)):
        chosen = chosen_list[level]
        sigma = jax.nn.sigmoid(chosen)
        slope = sigma * (1.0 + chosen * (1.0 - sigma))
        node_grad = node_grad + exact_dot(
            picks_t[level], own_gains[1 + level:2 + level, :] * slope * node_grad
        )
    final_grad[...] = node_grad
    final_state[...] = states

    def range_row(half, ball):
        return half * LOCAL + local_range * BALLS + ball

    def ng_copy():
        part = final_grad.at[pl.ds(pl.multiple_of(range_row(other_c, 0), BALLS), BALLS)]
        return send(part, node_grads.at[c], s_ng, 0, pair)

    ng_copy().start()
    for ball in range(BALLS):
        proj_copy(ball).start()
    node_grads[pl.ds(c, 1)] = final_grad[pl.ds(pl.multiple_of(range_row(c, 0), BALLS), BALLS), :][None]

    def own_mixed(ball, carry):
        state = final_state[pl.ds(range_row(c, ball), 1), :]
        mixed[ours(ball), :] = (hid[pl.ds(c, 1), here(ball), :][0] + state).astype(BF16)
        return carry

    lax.fori_loop(0, BALLS, own_mixed, 0)
    ng_copy().wait_recv()

    def backward(step, carry):
        rows = two(step)
        shifts = []
        for side in range(2):
            cot_copy(2 * step + side).wait_recv()
            row = pl.ds(2 * step + side, 1)
            shift = jnp.concatenate([node_grads[0, row, :], node_grads[1, row, :]], axis=1) * BALL ** (-0.5)
            shifts.append(jnp.broadcast_to(shift, (BALL, WIDTH)))
        hidden_grad = (both(cth, rows) + jnp.concatenate(shifts, axis=0)).astype(BF16)
        att_grad = nt(wo[...], hidden_grad).astype(BF16)
        value = vn[rows, :]
        prob_grads = [nn(value[sides[side], band], att_grad[band, sides[side]]) for side, band in pieces]
        acc_t[768:1024, :] += nn(att_t[step], hidden_grad)
        score_grads, halves = [], []
        for index in range(2 * HEADS):
            prob = probs[step * 2 * HEADS + index]
            dots = jnp.sum(prob_grads[index] * prob, axis=0, keepdims=True)
            score_grads.append((prob * (prob_grads[index] - dots) * SCALE).astype(BF16))
            halves.append(prob.astype(BF16))
        dv = [
            nt(att_grad[band, sides[side]], half).astype(BF16) for (side, band), half in zip(pieces, halves)
        ]
        dq = [
            nn(k_t[2 * step + side, band, :], part).astype(BF16)
            for (side, band), part in zip(pieces, score_grads)
        ]
        dk = [
            nt(q_t[2 * step + side, band, :], part).astype(BF16)
            for (side, band), part in zip(pieces, score_grads)
        ]
        all_grads = jnp.concatenate(
            [
                jnp.concatenate(dq[:HEADS] + dk[:HEADS] + dv[:HEADS], axis=0),
                jnp.concatenate(dq[HEADS:] + dk[HEADS:] + dv[HEADS:], axis=0),
            ],
            axis=1,
        )
        normed_grad = nn(wcat[...], all_grads)
        acc_t[0:768, :] += nn(all_grads, nrm[rows, :])
        scaled_grad = jnp.transpose(normed_grad) * gain
        ordered = both(xh, rows)
        inverse = jnp.concatenate([inv[rows, :], inv[rows, :]], axis=1)
        correction = jnp.sum(ordered * scaled_grad, axis=1, keepdims=True) * (1.0 / WIDTH)
        ordered_grad = (
            hidden_grad.astype(F32) + inverse * scaled_grad - ordered * (inverse * inverse * inverse) * correction
        ).astype(BF16)
        gstage[0, rows, :] = ordered_grad[:, :LOCAL]
        gstage[1, rows, :] = ordered_grad[:, LOCAL:]
        for side in range(2):
            grad_copy(2 * step + side).start()
        own = pl.ds(pl.multiple_of(c * HALF + step * 2 * BALL, 2 * BALL), 2 * BALL)
        grads[own, :] = gstage[pl.ds(c, 1), rows, :][0]
        return carry

    lax.fori_loop(0, BALLS // 2, backward, 0)

    for index in range(3):
        part = jnp.transpose(acc_t[index * 256:(index + 1) * 256, :])
        acc[0, index * 256:(index + 1) * 256, :] = part[:, :LOCAL]
        acc[1, index * 256:(index + 1) * 256, :] = part[:, LOCAL:]
    for half in range(2):
        band = slice(768 + half * LOCAL, 768 + (half + 1) * LOCAL)
        acc[half, 768:896, :] = acc_t[band, :LOCAL]
        acc[half, 896:1024, :] = acc_t[band, LOCAL:]

    kept = pl.ds(pl.multiple_of(core * 512, 512), 512)
    given = pl.ds(pl.multiple_of((1 - core) * 512, 512), 512)
    copy_a = send(acc.at[:, given], recv_a, s_a, 0, sibling)
    copy_a.start()

    tiles = ROWS // LOCAL
    lanes = lax.broadcasted_iota(jnp.int32, (1, LOCAL), 1)
    high_ids = lax.broadcasted_iota(jnp.int32, (tiles, LOCAL), 0)
    low_ids = lax.broadcasted_iota(jnp.int32, (LOCAL, LOCAL), 0)
    high_hits, low_hits = [], []
    for tile in range(tiles):
        target = order_rows[tile:tile + 1, :]
        high_hits.append(jnp.where(high_ids == target // LOCAL, 1.0, 0.0).astype(BF16))
        hit = low_ids == target % LOCAL
        source = lanes + tile * LOCAL
        low_hits.append(
            jnp.concatenate(
                [
                    jnp.where(hit, (source // 64).astype(F32), 0.0),
                    jnp.where(hit, (source % 64).astype(F32), 0.0),
                ],
                axis=0,
            ).astype(BF16)
        )
    found = nt(jnp.concatenate(high_hits, axis=1), jnp.concatenate(low_hits, axis=1))
    inverse_order = (found[:, :LOCAL] * 64.0 + found[:, LOCAL:]).astype(jnp.int32)
    places[...] = jnp.clip(inverse_order, 0, ROWS - 1)
    fetch = pltpu.make_async_copy(places, places_smem, s_places)
    fetch.start()

    def return_rows(start, stop):
        def step(block, carry):
            for inner in range(16):
                row = places_smem[block // 8, (block % 8) * 16 + inner]
                moved[pl.ds(block * 16 + inner, 1), :] = wide[pl.ds(row, 1), :]
            return carry

        lax.fori_loop(start // 16, stop // 16, step, 0)
        point_grad[start:stop, :] = moved[start:stop, :].astype(BF16)

    def their_mixed(ball, carry):
        rows = here(ball)
        proj_copy(ball).wait_recv()
        state = final_state[pl.ds(range_row(other_c, ball), 1), :]
        mixed[theirs(ball), :] = (
            theirs_rows[rows, :].astype(F32) + precv[rows, :].astype(F32) + state
        ).astype(BF16)
        return carry

    copy_a.wait_recv()
    sum_a[...] = acc[:, kept, :] + recv_a[...]
    half_a[...] = sum_a[...].astype(BF16)

    def copy_c(distance):
        piece = pl.ds(pl.multiple_of(plane_index(distance) * 32, 32), 32)
        return send(half_a.at[:, piece], recv_c.at[distance], s_c, distance, plane_peer(distance))

    for distance in range(1, 16):
        copy_c(distance).start()
    lax.fori_loop(0, BALLS, their_mixed, 0)
    part = sum_a[:, pl.ds(pl.multiple_of(plane * 32, 32), 32), :]
    for distance in range(1, 16):
        copy_c(distance).wait_recv()
        part = part + recv_c[distance].astype(F32)
    sum_c[...] = part

    def copy_z(distance):
        return send(sum_c.at[(ring + distance) % 2], recv_z.at[ring], s_z, distance, ring_peer(distance))

    for distance in range(1, 8):
        copy_z(distance).start()
    recv_z[pl.ds(ring, 1)] = sum_c[pl.ds(c, 1)]
    for ball in range(BALLS):
        grad_copy(ball).wait_recv()
    wide[...] = grads[...].astype(F32)
    fetch.wait()
    return_rows(0, HALF)
    for distance in range(1, 8):
        copy_z(distance).wait_recv()
    part = recv_z[0]
    for step in range(1, 8):
        part = part + recv_z[step]
    plane_rows = pl.ds(pl.multiple_of(plane * 32, 32), 32)
    all_f[plane_rows, :] = part

    def copy_f(distance):
        return send(all_f.at[plane_rows], all_f.at[plane_rows], s_f, distance, plane_peer(distance))

    for distance in range(1, 16):
        copy_f(distance).start()
    return_rows(HALF, ROWS)

    small_copy().wait_send()
    ng_copy().wait_send()

    def settle_early(ball, carry):
        points_copy(ball).wait_send()
        cot_copy(ball).wait_send()
        return carry

    lax.fori_loop(0, BALLS, settle_early, 0)
    tree_first().wait_send()
    early_first().wait_send()
    for distance in range(1, 8):
        early_copy(distance).wait_send()
    for distance in range(1, 16):
        tree_copy(distance).wait_send()
        copy_c(distance).wait_send()

    for distance in range(1, 16):
        copy_f(distance).wait_recv()

    copy_g = send(all_f, total.at[kept], s_g, 0, sibling)
    copy_g.start()
    total[kept, :] = all_f[...]
    copy_g.wait_recv()
    for index in range(3):
        qkv_out[index] = total[index * 256:(index + 1) * 256, :]
    out_out[:, :LOCAL] = total[768:896, :]
    out_out[:, LOCAL:] = total[896:1024, :]

    def settle(ball, carry):
        proj_copy(ball).wait_send()
        grad_copy(ball).wait_send()
        return carry

    lax.fori_loop(0, BALLS, settle, 0)
    copy_a.wait_send()
    for distance in range(1, 16):
        copy_f(distance).wait_send()
    for distance in range(1, 8):
        copy_z(distance).wait_send()
    copy_g.wait_send()


def run_main(order, order_rows, points, cot, gain, tree_gain, slots, w, wo):
    vmem = pl.BlockSpec(memory_space=pltpu.VMEM)
    sems = lambda count: pltpu.SemaphoreType.DMA((2, count))
    v = pltpu.VMEM
    return pl.pallas_call(
        main_kernel,
        out_shape=(
            jax.ShapeDtypeStruct((ROWS, LOCAL), BF16),
            jax.ShapeDtypeStruct((ROWS, LOCAL), BF16),
            jax.ShapeDtypeStruct((3, WIDTH, LOCAL), F32),
            jax.ShapeDtypeStruct((LOCAL, WIDTH), F32),
        ),
        in_specs=[pl.BlockSpec(memory_space=pltpu.SMEM)] + [vmem] * 8,
        out_specs=(vmem,) * 4,
        scratch_shapes=[
            v((ROWS, LOCAL), F32),
            v((ROWS, LOCAL), F32),
            v((HALF, LOCAL), BF16),
            v((2, HALF, LOCAL), BF16),
            v((2, HALF, LOCAL), BF16),
            v((2, 8, LOCAL), F32),
            v((3, WIDTH, WIDTH), BF16),
            v((WIDTH, 3 * WIDTH), BF16),
            v((HALF, WIDTH), BF16),
            v((BALLS, WIDTH, BALL), BF16),
            v((BALLS, WIDTH, BALL), BF16),
            v((BALLS // 2, WIDTH, 2 * BALL), BF16),
            v((HALF, WIDTH), BF16),
            v((2, HALF, LOCAL), F32),
            v((HALF, LOCAL), F32),
            v((BALLS * HEADS, BALL, BALL), F32),
            v((2, LOCAL, 2 * LOCAL), F32),
            v((2, 16, LOCAL), F32),
            v((2, LOCAL, LOCAL), F32),
            v((LEVELS, 256, 256), BF16),
            v((LEVELS, 256, 256), BF16),
            v((256, LOCAL), F32),
            v((256, LOCAL), F32),
            v((2, BALLS, LOCAL), F32),
            v((2, HALF, LOCAL), BF16),
            v((HALF, LOCAL), BF16),
            v((2, HALF, LOCAL), BF16),
            v((1024, WIDTH), F32),
            v((2, 1024, LOCAL), F32),
            v((2, 512, LOCAL), F32),
            v((2, 512, LOCAL), F32),
            v((2, 512, LOCAL), BF16),
            v((16, 2, 32, LOCAL), BF16),
            v((2, 32, LOCAL), F32),
            v((8, 32, LOCAL), F32),
            v((512, LOCAL), F32),
            v((1024, LOCAL), F32),
            v((ROWS, LOCAL), BF16),
            v((ROWS // LOCAL, LOCAL), jnp.int32),
            pltpu.SMEM((ROWS // LOCAL, LOCAL), jnp.int32),
            pltpu.SemaphoreType.DMA,
            sems(1), sems(BALLS), sems(BALLS), sems(BALLS), sems(BALLS), sems(8), sems(16),
            sems(1), sems(1), sems(16), sems(8), sems(16), sems(1),
        ],
        compiler_params=pltpu.CompilerParams(
            collective_id=0, has_side_effects=True, vmem_limit_bytes=58 * 1024 * 1024
        ),
        cost_estimate=pl.CostEstimate(flops=8 * 10**9, bytes_accessed=8 * 10**6, transcendentals=4 * 10**6),
    )(order, order_rows, points, cot, gain, tree_gain, slots, w, wo)


def local(points, order, norm_gain, qkv_weight, out_weight, tree_gain, partner_slot, cotangent):
    return run_main(
        order, order.reshape(ROWS // LOCAL, LOCAL), points, cotangent, norm_gain[None], tree_gain,
        partner_slot.T, qkv_weight, out_weight,
    )


def solution(mesh):
    in_specs = (
        P("pts", "ch"),
        P("pts"),
        P("ch"),
        P(),
        P(),
        P(None, "ch"),
        P("pts", None),
        P("pts", "ch"),
    )
    out_specs = (P("pts", "ch"), P("pts", "ch"), P(None, None, "ch"), P("ch", None))
    return jax.shard_map(local, mesh=mesh, in_specs=in_specs, out_specs=out_specs, check_vma=False)
```
